256 devices in a mesh: gx: 8 (over y, core), gy: 8 (over z), gz: 4 (over x).
Axes of the slice: x: 4, y: 4, z: 8, core: 2. Of those that a mesh axis runs over, the one named last changes fastest.
Arguments:
- positions: float32 [3, 65536], P(None, ('gx', 'gy', 'gz')), may hold values from 0 to 3
- features: bfloat16 [64, 65536], P(None, ('gx', 'gy', 'gz')), may hold values from -6 to 6
- ghost_rows: int32 [32768], P(('gx', 'gy', 'gz')), may hold values from 0 to 255, as said below
- pair_center: int32 [786432], P(('gx', 'gy', 'gz')), may hold values from 0 to 255, as said below
- pair_nbr: int32 [786432], P(('gx', 'gy', 'gz')), may hold values from 0 to 3711, as said below
- pair_count: int32 [256], P(('gx', 'gy', 'gz')), may hold values from 1536 to 3072, as said below
- emb_weight: float32 [136, 64], replicated, may hold values from -0.5 to 0.5
- value_weight: float32 [64, 64], replicated, may hold values from -0.75 to 0.75
- env_weight: float32 [2, 64, 64], replicated, may hold values from -0.75 to 0.75
- path_weight: float32 [2, 7, 64], replicated, may hold values from 0.5 to 1.5
- latent_weight: float32 [2, 256, 64], replicated, may hold values from -0.375 to 0.375
- gate_weight: float32 [1, 64, 64], replicated, may hold values from -0.75 to 0.75
- final_weight: float32 [64, 64], replicated, may hold values from -0.75 to 0.75
- out_weight: float32 [64], replicated, may hold values from -0.75 to 0.75
Outputs:
- site_energy: float32 [65536], P(('gx', 'gy', 'gz'))
- forces: float32 [3, 65536], P(None, ('gx', 'gy', 'gz'))
The draws below stay inside these ranges and needn't reach their ends.
Inputs may be any that keep to these rules, and one draw needn't show every extreme that they name: `ghost_rows`: the 128 entries of one block are distinct block-local atom indices. `pair_center`: block-local atom indices. `pair_nbr`: an index below 256 is an own atom other than the center; else it is 256 + k * 128 + r with slot k never 13. `pair_count`: some block is full in every draw.
All inputs are finite; a program needn't handle non-finite values.
Results may differ from the reference program's by a relative error of at most 0.0004.
Values sent between devices are 32-bit elements; how exact they have to be, the bound alone decides.
A program may use at most 192 MiB of HBM per device.

```python
import jax
import jax.numpy as jnp
import numpy as np
from jax import lax

C = 64
NB = 8
LAYERS = 2
A_DEV = 256
GHOSTS = 128
P_CAP = 3072
BLOCKS = 256
ATOMS = 65536
N_GX = 8
N_GY = 8
N_GZ = 4


def slot_table():
    entries = []
    for slot in range(27):
        if slot == 13:
            continue
        moved = int(slot // 9 != 1) + int(slot // 3 % 3 != 1) + int(slot % 3 != 1)
        entries = entries + [slot] * 2 ** (3 - moved)
    return np.array(entries, dtype=np.int32)


def pair_lists(key):
    table = jnp.asarray(slot_table())
    centers = jax.random.randint(jax.random.fold_in(key, 11), (BLOCKS, P_CAP), 0, A_DEV)
    kind = jax.random.randint(jax.random.fold_in(key, 12), (BLOCKS, P_CAP), 0, 2)
    step = jax.random.randint(jax.random.fold_in(key, 13), (BLOCKS, P_CAP), 1, A_DEV)
    local = (centers + step) % A_DEV
    pick = jax.random.randint(jax.random.fold_in(key, 14), (BLOCKS, P_CAP), 0, table.shape[0])
    direction = table[pick]
    moved = (direction // 9 != 1).astype(jnp.int32) + (direction // 3 % 3 != 1).astype(jnp.int32) + (direction % 3 != 1).astype(jnp.int32)
    limit = jnp.right_shift(jnp.full_like(moved, GHOSTS), moved - 1)
    draws = jax.random.randint(jax.random.fold_in(key, 15), (BLOCKS, P_CAP), 0, 2 ** 20)
    row = draws % limit
    ghost = A_DEV + direction * GHOSTS + row
    neighbour = jnp.where(kind == 0, local, ghost)
    return (centers.reshape(-1).astype(jnp.int32), neighbour.reshape(-1).astype(jnp.int32))


def draw_pair_center(key, part):
    return pair_lists(key)[0]


def draw_pair_nbr(key, part):
    return pair_lists(key)[1]


def draw_ghost_rows(key, part):
    key = jax.random.fold_in(key, 3)
    scores = jax.random.randint(key, (BLOCKS, A_DEV), 0, 2 ** 20) * A_DEV + jnp.arange(A_DEV, dtype=jnp.int32)[None, :]
    order = jnp.argsort(scores, axis=1, stable=True)
    return order[:, :GHOSTS].reshape(-1).astype(jnp.int32)


def draw_pair_count(key, part):
    key = jax.random.fold_in(key, 5)
    counts = jax.random.randint(jax.random.fold_in(key, 1), (BLOCKS,), P_CAP // 2, P_CAP + 1)
    full = jax.random.randint(jax.random.fold_in(key, 2), (), 0, BLOCKS)
    return jnp.where(jnp.arange(BLOCKS, dtype=jnp.int32) == full, P_CAP, counts).astype(jnp.int32)


def steps_of(rng, dims, split, least, top_value):
    gain, own = 1.0, jax.random.fold_in(rng, 6)
    for dim, shards_of in split:
        steps = jnp.exp(jax.random.uniform(jax.random.fold_in(own, dim), (shards_of,), jnp.float32, least / len(split), top_value / len(split)))
        gain = gain * jnp.repeat(steps, dims[dim] // shards_of).reshape([-1 if axis == dim else 1 for axis in range(len(dims))])
    return gain


def normal_values(own_key, dims, scale, most, pieces=(), held_as=jnp.bfloat16):
    values = scale * jax.random.normal(own_key, dims, jnp.float32)
    if pieces:
        values = values * steps_of(own_key, dims, pieces, -0.22, 0.18)
    return jnp.clip(values, -most, most).astype(held_as)


def setup_inputs(seed: int = 0) -> dict:
    splits = jax.random.split(jax.random.key(seed), 15)
    return {
        "positions": jnp.clip(3.0 * jax.random.uniform(splits[0], (3, ATOMS), jnp.float32) ** steps_of(splits[0], (3, ATOMS), ((1, 256),), -0.2, 0.2), 0.0, 3.0),
        "features": normal_values(splits[1], (C, ATOMS), 1.0, 6.0, ((1, 256),)),
        "ghost_rows": draw_ghost_rows(jax.random.fold_in(splits[14], 71), 0),
        "pair_center": draw_pair_center(jax.random.fold_in(splits[14], 71), 0),
        "pair_nbr": draw_pair_nbr(jax.random.fold_in(splits[14], 71), 0),
        "pair_count": draw_pair_count(jax.random.fold_in(splits[14], 71), 0),
        "emb_weight": normal_values(splits[6], (2 * C + NB, C), (2 * C + NB) ** -0.5, 0.5, (), jnp.float32),
        "value_weight": normal_values(splits[7], (C, C), C ** -0.5, 0.75, (), jnp.float32),
        "env_weight": normal_values(splits[8], (LAYERS, C, C), C ** -0.5, 0.75, (), jnp.float32),
        "path_weight": jnp.clip(jax.random.uniform(splits[9], (LAYERS, 7, C), jnp.float32, 0.5, 1.5), 0.5, 1.5),
        "latent_weight": normal_values(splits[10], (LAYERS, 4 * C, C), (4 * C) ** -0.5, 0.375, (), jnp.float32),
        "gate_weight": normal_values(splits[11], (LAYERS - 1, C, C), C ** -0.5, 0.75, (), jnp.float32),
        "final_weight": normal_values(splits[12], (C, C), C ** -0.5, 0.75, (), jnp.float32),
        "out_weight": normal_values(splits[13], (C,), C ** -0.5, 0.75, (), jnp.float32),
    }


edge_length = 3.0
env_scale = 0.125
root_three = 1.7320508075688772

def matmul(weight, data):
    return jnp.dot(weight.T, data, precision=lax.Precision.HIGHEST)

def slot_offsets():
    slots = jnp.arange(27, dtype=jnp.int32)
    return jnp.stack([slots // 9 - 1, slots // 3 % 3 - 1, slots % 3 - 1]).astype(jnp.float32) * edge_length

def site_energies(local_pos, ghost_pos, local_feat, ghost_feat, center, neighbour, count, params):
    emb_weight, value_weight, env_weight, path_weight, latent_weight, gate_weight, final_weight, out_weight = params
    atoms = local_pos.shape[1]
    slots = center.shape[0]
    all_pos = jnp.concatenate([local_pos, ghost_pos], 1)
    all_feat = jnp.concatenate([local_feat, ghost_feat], 1)
    delta = all_pos[:, neighbour] - all_pos[:, center]
    radius = jnp.sqrt(lax.optimization_barrier(jnp.sum(delta * delta, 0)) + 1.0)
    unit = delta / radius
    ux, uy, uz = (unit[0], unit[1], unit[2])
    harmonic = jnp.stack([jnp.ones_like(ux), ux, uy, uz, root_three * ux * uy, root_three * uy * uz, root_three * uz * ux, root_three * 0.5 * (ux * ux - uy * uy), 0.5 * (2.0 * uz * uz - ux * ux - uy * uy)])
    live = (jnp.arange(slots, dtype=jnp.int32) < count).astype(jnp.float32)
    centers_mu = jnp.arange(emb_weight.shape[0] - 2 * local_feat.shape[0], dtype=jnp.float32) * 1.25
    basis = jnp.exp(-0.5 * (radius[None, :] - centers_mu[:, None]) ** 2)
    joined = jnp.concatenate([all_feat[:, center], all_feat[:, neighbour], basis], 0)
    latent = jax.nn.silu(matmul(emb_weight, joined))
    tensor = matmul(value_weight, latent)[None] * harmonic[:, None]
    layers = env_weight.shape[0]
    for layer in range(layers):
        embed = matmul(env_weight[layer], latent) * live[None]
        message = embed[None] * harmonic[:, None]
        chans = latent.shape[0]
        gamma = jnp.zeros((9, chans, atoms), jnp.float32).at[:, :, center].add(message) * env_scale
        beside_all = gamma[:, :, center]
        weights = path_weight[layer][:, :, None]
        scalar0 = tensor[0] * beside_all[0]
        scalar1 = lax.optimization_barrier(jnp.sum(tensor[1:4] * beside_all[1:4], 0))
        scalar2 = lax.optimization_barrier(jnp.sum(tensor[4:] * beside_all[4:], 0))
        mixed = jnp.concatenate([latent, weights[0] * scalar0, weights[1] * scalar1, weights[2] * scalar2], 0)
        latent = latent + jax.nn.silu(matmul(latent_weight[layer], mixed))
        if layer < layers - 1:
            gating = matmul(gate_weight[layer], latent)
            part0 = (weights[0] * scalar0 + weights[1] * scalar1 + weights[2] * scalar2)[None]
            part1 = weights[3] * tensor[0][None] * beside_all[1:4] + weights[4] * tensor[1:4] * beside_all[0][None]
            part2 = weights[5] * tensor[0][None] * beside_all[4:] + weights[6] * tensor[4:] * beside_all[0][None]
            tensor = jnp.concatenate([part0, part1, part2], 0) * gating[None]
    hidden = jax.nn.silu(matmul(final_weight, latent))
    energy = jnp.dot(out_weight, hidden, precision=lax.Precision.HIGHEST) * live
    return jnp.zeros((atoms,), jnp.float32).at[center].add(energy)

def energy_grads(local_pos, ghost_pos, local_feat, ghost_feat, center, neighbour, count, params):

    def total(first, second):
        site = site_energies(first, second, local_feat, ghost_feat, center, neighbour, count, params)
        return (jnp.sum(site), site)
    value, pullback, site = jax.vjp(total, local_pos, ghost_pos, has_aux=True)
    local_grad, ghost_grad = pullback(jnp.ones((), jnp.float32))
    return (local_grad, ghost_grad, site)

def reference(positions, features, ghost_rows, pair_center, pair_nbr, pair_count, emb_weight, value_weight, env_weight, path_weight, latent_weight, gate_weight, final_weight, out_weight):
    params = (emb_weight, value_weight, env_weight, path_weight, latent_weight, gate_weight, final_weight, out_weight)
    blocks = N_GX * N_GY * N_GZ
    feats = features.astype(jnp.float32)
    slots = jnp.arange(27, dtype=jnp.int32)
    shift_a, shift_b, shift_c = (slots // 9 - 1, slots // 3 % 3 - 1, slots % 3 - 1)
    offsets = slot_offsets()
    table_rows = ghost_rows.reshape(blocks, GHOSTS)
    centers_all = pair_center.reshape(blocks, P_CAP)
    nbrs_all = pair_nbr.reshape(blocks, P_CAP)

    def one_block(forces, block):
        bx = block // (N_GY * N_GZ)
        by = block // N_GZ % N_GY
        bz = block % N_GZ
        source = ((bx + shift_a) % N_GX * N_GY + (by + shift_b) % N_GY) * N_GZ + (bz + shift_c) % N_GZ
        rows = table_rows[source]
        index = (source[:, None] * A_DEV + rows).reshape(-1).astype(jnp.int32)
        ghost_pos = (positions[:, index].reshape(3, 27, GHOSTS) + offsets[:, :, None]).reshape(3, 27 * GHOSTS)
        ghost_feat = feats[:, index]
        start = (block * A_DEV).astype(jnp.int32)
        local_pos = lax.dynamic_slice_in_dim(positions, start, A_DEV, 1)
        local_feat = lax.dynamic_slice_in_dim(feats, start, A_DEV, 1)
        local_grad, ghost_grad, site = energy_grads(local_pos, ghost_pos, local_feat, ghost_feat, centers_all[block], nbrs_all[block], pair_count[block], params)
        own = start + jnp.arange(A_DEV, dtype=jnp.int32)
        forces = forces.at[:, own].add(-local_grad).at[:, index].add(-ghost_grad)
        return (forces, site)
    forces, sites = lax.scan(one_block, jnp.zeros((3, A_DEV * blocks), jnp.float32), jnp.arange(blocks, dtype=jnp.int32))
    return (sites.reshape(-1), forces)
```

```python
import functools

import jax
import jax.numpy as jnp
from jax import lax
from jax.experimental import pallas as pl
from jax.experimental.pallas import tpu as pltpu
from jax.sharding import PartitionSpec as P

edge_length = 3.0
env_scale = 0.125
root_three = 1.7320508075688772
axes = ("gx", "gy", "gz")
MESH = pl.DeviceIdType.MESH
f32 = jnp.float32
bf16 = jnp.bfloat16
C = 64
SLOTS = [k for k in range(27) if k != 13]
ROWS = 72
TILE = 256


def offset(k):
    return (k // 9 - 1, k // 3 % 3 - 1, k % 3 - 1)


def peer(k, sign):
    me = [lax.axis_index(a) for a in axes]
    sizes = [lax.axis_size(a) for a in axes]
    return tuple(lax.rem(m + sign * o + s, s) for m, o, s in zip(me, offset(k), sizes))


def greet():
    barrier = pltpu.get_barrier_semaphore()
    for k in SLOTS:
        pl.semaphore_signal(barrier, inc=1, device_id=peer(k, 1), device_id_type=MESH)
    pl.semaphore_wait(barrier, len(SLOTS))


def dot(a, b):
    return jnp.dot(a, b, preferred_element_type=f32)


def dot_nt(a, b):
    return lax.dot_general(a, b, (((1,), (1,)), ((), ())), preferred_element_type=f32)


def hi(x):
    return x.astype(bf16).astype(f32)


def halves(x):
    first = x.astype(bf16)
    return first, (x - first.astype(f32)).astype(bf16)


def thirds(x):
    first = hi(x)
    rest = x - first
    second = hi(rest)
    return first, second, rest - second


def halo_kernel(pos_ref, feat_ref, rows_ref, out_ref, send_buf, send_sem, recv_sem):
    greet()
    atoms = feat_ref.shape[1]
    sent = rows_ref.shape[1]
    pick = (
        lax.broadcasted_iota(jnp.int32, (atoms, sent), 0)
        == jnp.broadcast_to(rows_ref[...], (atoms, sent))
    ).astype(bf16)
    send_buf[0:C, :] = dot(feat_ref[...], pick)
    parts = thirds(pos_ref[...])
    send_buf[C : C + 3, :] = (
        dot(parts[0].astype(bf16), pick)
        + dot(parts[1].astype(bf16), pick)
        + dot(parts[2].astype(bf16), pick)
    )
    send_buf[C + 3 : ROWS, :] = jnp.zeros((ROWS - C - 3, sent), f32)
    copies = []
    for k in SLOTS:
        copy = pltpu.make_async_remote_copy(
            src_ref=send_buf,
            dst_ref=out_ref.at[k],
            send_sem=send_sem.at[k],
            recv_sem=recv_sem.at[k],
            device_id=peer(k, -1),
            device_id_type=MESH,
        )
        copy.start()
        copies.append(copy)
    out_ref[13] = jnp.zeros((ROWS, sent), f32)
    for copy in copies:
        copy.wait()


def halo(positions, features, rows):
    sent = rows.shape[1]
    return pl.pallas_call(
        halo_kernel,
        out_shape=jax.ShapeDtypeStruct((27, ROWS, sent), f32),
        in_specs=[pl.BlockSpec(memory_space=pltpu.VMEM)] * 3,
        out_specs=pl.BlockSpec(memory_space=pltpu.VMEM),
        scratch_shapes=[
            pltpu.VMEM((ROWS, sent), f32),
            pltpu.SemaphoreType.DMA((27,)),
            pltpu.SemaphoreType.DMA((27,)),
        ],
        compiler_params=pltpu.CompilerParams(collective_id=0, has_side_effects=True),
    )(positions, features, rows)


def return_kernel(ghost_ref, own_ref, rows_ref, force_ref, landed, send_sem, recv_sem):
    greet()
    copies = []
    for k in SLOTS:
        copy = pltpu.make_async_remote_copy(
            src_ref=ghost_ref.at[k],
            dst_ref=landed.at[k],
            send_sem=send_sem.at[k],
            recv_sem=recv_sem.at[k],
            device_id=peer(k, 1),
            device_id_type=MESH,
        )
        copy.start()
        copies.append(copy)
    atoms = own_ref.shape[1]
    sent = rows_ref.shape[1]
    pick = (
        lax.broadcasted_iota(jnp.int32, (atoms, sent), 0)
        == jnp.broadcast_to(rows_ref[...], (atoms, sent))
    ).astype(bf16)
    for copy in copies:
        copy.wait()
    owned = landed[SLOTS[0]]
    for k in SLOTS[1:]:
        owned = owned + landed[k]
    parts = thirds(owned)
    back = (
        dot_nt(parts[0].astype(bf16), pick)
        + dot_nt(parts[1].astype(bf16), pick)
        + dot_nt(parts[2].astype(bf16), pick)
    )
    force_ref[...] = -(own_ref[...] + back[0:3, :])


def give_back(ghost_grad, own_grad, rows):
    sent = rows.shape[1]
    return pl.pallas_call(
        return_kernel,
        out_shape=jax.ShapeDtypeStruct(own_grad.shape, f32),
        in_specs=[pl.BlockSpec(memory_space=pltpu.VMEM)] * 3,
        out_specs=pl.BlockSpec(memory_space=pltpu.VMEM),
        scratch_shapes=[
            pltpu.VMEM((27, 8, sent), f32),
            pltpu.SemaphoreType.DMA((27,)),
            pltpu.SemaphoreType.DMA((27,)),
        ],
        compiler_params=pltpu.CompilerParams(collective_id=1, has_side_effects=True),
    )(ghost_grad, own_grad, rows)


def forward_stack(weight):
    first = hi(weight)
    return jnp.concatenate([first, first, weight - first], 0).T.astype(bf16)


def backward_stack(weight):
    first = hi(weight)
    return jnp.concatenate([first, first, weight - first], 1).astype(bf16)


def stacked(x):
    first, second = halves(x)
    return jnp.concatenate([first, second, first], 0)


def sigmoid(x):
    return 0.5 * jnp.tanh(0.5 * x) + 0.5


def fold(x):
    total = x[0:8]
    for i in range(1, C // 8):
        total = total + x[8 * i : 8 * i + 8]
    return total


def chan(m):
    return slice(m * C, (m + 1) * C)


def pair_kernel(
    table_ref, pos_ref, feat_ref, center_ref, nbr_ref, count_ref,
    emb_ref, value_ref, env_ref, path_ref, latent_ref, gate_ref, final_ref, out_ref,
    site_ref, own_ref, ghost_ref,
    w_emb, w_ve, w_ge, w_fin, w_finb, w_lat, w_latb, w_b1, w_b0, w_embb, w_path, w_out,
    tab_feat, tab_pos, tab_pos3, tab_own,
    hot, hot_t, near, slot_s, geo, harm, basis_s,
    x_s, xh_s, xl_s, d0_s, d1_s, v_s, g_s, e0_s, e1_s, t1_s, t2_s,
    dx_s, dv_s, dg_s, dg0_s, dt1_s, dt2_s, k1_s, k2_s, j1_s, j2_s, dy_s, eps_s,
    big_g, big_h, work, msg_h, msg_l, acc, cat, acc_own, acc_near,
):
    pairs = center_ref.shape[1]
    atoms = pos_ref.shape[1]
    T = TILE
    steps = pairs // T

    emb = emb_ref[...]
    emb_h = hi(emb)
    emb_l = emb - emb_h
    w_emb[...] = jnp.concatenate(
        [
            jnp.concatenate([emb_h, emb_h[2 * C :]], 0),
            jnp.concatenate([emb_l, jnp.zeros((8, C), f32)], 0),
        ],
        1,
    ).T.astype(bf16)
    w_embb[...] = backward_stack(emb[2 * C :])
    w_ve[...] = forward_stack(jnp.concatenate([value_ref[...], env_ref[0]], 1))
    w_ge[...] = forward_stack(jnp.concatenate([gate_ref[0], env_ref[1]], 1))
    w_b0[...] = backward_stack(jnp.concatenate([env_ref[0], value_ref[...]], 1))
    w_b1[...] = backward_stack(jnp.concatenate([env_ref[1], gate_ref[0]], 1))
    w_fin[...] = forward_stack(final_ref[...])
    w_finb[...] = backward_stack(final_ref[...])
    w_out[...] = jnp.broadcast_to(out_ref[...], (8, C)).T
    for layer in range(2):
        cols = jnp.concatenate([path_ref[layer], jnp.ones((1, C), f32)], 0).T
        if layer == 0:
            w_path[...] = cols
        scaled = jnp.concatenate(
            [latent_ref[layer, 0:C]]
            + [latent_ref[layer, chan(i + 1)] * cols[:, i : i + 1] for i in range(3)],
            0,
        )
        first = hi(scaled)
        w_lat[layer] = jnp.concatenate([first, scaled - first], 1).T.astype(bf16)
        w_latb[layer] = backward_stack(scaled)

    tab_pos[...] = jnp.zeros(tab_pos.shape, f32)
    tab_feat[0:C, :] = feat_ref[:, 0:128]
    tab_feat[C : 2 * C, :] = feat_ref[:, 128:256]
    for k in range(27):
        tab_feat[(k + 2) * C : (k + 3) * C, :] = table_ref[k, 0:C, :].astype(bf16)
    for c in range(3):
        tab_pos[c * 32 : c * 32 + 1, :] = pos_ref[c : c + 1, 0:128]
        tab_pos[c * 32 + 1 : c * 32 + 2, :] = pos_ref[c : c + 1, 128:256]
        for k in range(27):
            tab_pos[c * 32 + k + 2 : c * 32 + k + 3, :] = (
                table_ref[k, C + c : C + c + 1, :] + edge_length * offset(k)[c]
            )
    for i, part in enumerate(thirds(tab_pos[...])):
        tab_pos3[i * 96 : (i + 1) * 96, :] = part.astype(bf16)
    tab_own[0:C, :] = feat_ref[...]
    tab_own[C : C + 16, :] = jnp.concatenate(
        list(thirds(pos_ref[...])) + [jnp.zeros((7, atoms), f32)], 0
    ).astype(bf16)

    def span(t):
        return pl.ds(pl.multiple_of(t * T, T), T)

    def live_at(t):
        at = lax.broadcasted_iota(jnp.int32, (1, T), 1) + t * T
        return jnp.where(at < jnp.broadcast_to(count_ref[...], (1, T)), 1.0, 0.0)

    def scatter(t):
        return dot(msg_h[...], hot[span(t), :]) + dot(msg_l[...], hot[span(t), :])

    def put(m, x):
        first, second = halves(x)
        msg_h[chan(m), :] = first
        msg_l[chan(m), :] = second

    def make_cat():
        first, second = halves(acc[...])
        cat[:, 0:atoms] = first
        cat[:, atoms : 2 * atoms] = second

    def latent(layer, xh, xl, scalars):
        split = [halves(s) for s in scalars]
        high = jnp.concatenate([xh] + [s[0] for s in split], 0)
        low = jnp.concatenate([xl] + [s[1] for s in split], 0)
        both = dot(w_lat[layer], high)
        return both[0:C] + both[C:] + dot(w_lat[layer, 0:C], low)

    def phase_a(t, carry):
        at = span(t)
        nbr = nbr_ref[:, at]
        rest = jnp.bitwise_and(nbr, 127)
        slot = jnp.right_shift(nbr, 7)
        r = (
            lax.broadcasted_iota(jnp.int32, (128, T), 0) == jnp.broadcast_to(rest, (128, T))
        ).astype(bf16)
        near[:, at] = r
        s = jnp.where(
            lax.broadcasted_iota(jnp.int32, (32, T), 0) == jnp.broadcast_to(slot, (32, T)), 1.0, 0.0
        )
        slot_s[:, at] = s
        own = (
            lax.broadcasted_iota(jnp.int32, (atoms, T), 0)
            == jnp.broadcast_to(center_ref[:, at], (atoms, T))
        ).astype(f32)
        hot_t[0:atoms, at] = own.astype(bf16)
        hot_t[atoms : 2 * atoms, at] = own.astype(bf16)
        hot[at, :] = own.T.astype(bf16)
        found = dot(tab_own[...], hot_t[0:atoms, at])
        feat_i = found[0:C]
        pos_i = found[C : C + 3] + found[C + 3 : C + 6] + found[C + 6 : C + 9]
        far = dot(tab_pos3[...], r)
        far = far[0:96] + far[96:192] + far[192:288]
        pos_j = jnp.concatenate(
            [jnp.sum(far[c * 32 : c * 32 + 32] * s, 0, keepdims=True) for c in range(3)], 0
        )
        feat_j = jnp.zeros((C, T), f32)
        for k0 in range(0, 29, 8):
            many = min(8, 29 - k0)
            got = dot(tab_feat[k0 * C : (k0 + many) * C, :], r)
            for k in range(many):
                feat_j = feat_j + got[chan(k)] * s[k0 + k : k0 + k + 1]
        d = pos_j - pos_i
        rho = jnp.sqrt(jnp.sum(d * d, 0, keepdims=True) + 1.0)
        inv = 1.0 / rho
        u = d * inv
        ux, uy, uz = u[0:1], u[1:2], u[2:3]
        y = [
            None, ux, uy, uz,
            root_three * ux * uy,
            root_three * uy * uz,
            root_three * uz * ux,
            (root_three * 0.5) * (ux * ux - uy * uy),
            0.5 * (2.0 * uz * uz - ux * ux - uy * uy),
        ]
        for m in range(1, 9):
            harm[m : m + 1, at] = y[m]
        geo[0:3, at] = u
        geo[3:4, at] = rho
        mu = lax.broadcasted_iota(jnp.int32, (8, T), 0).astype(f32) * 1.25
        z = rho - mu
        basis = jnp.exp(-0.5 * z * z)
        basis_s[:, at] = basis * z
        joined = jnp.concatenate(
            [
                feat_i.astype(bf16),
                feat_j.astype(bf16),
                jnp.concatenate([basis, basis - hi(basis)], 0).astype(bf16),
            ],
            0,
        )
        pre = dot(w_emb[...], joined)
        pre = pre[0:C] + pre[C:]
        sg = sigmoid(pre)
        x = pre * sg
        d0_s[:, at] = sg * (1.0 + pre * (1.0 - sg))
        xh, xl = halves(x)
        x_s[:, at] = x
        xh_s[:, at] = xh
        xl_s[:, at] = xl
        ve = dot(w_ve[...], jnp.concatenate([xh, xl, xh], 0))
        v_s[:, at] = ve[0:C]
        e = ve[C:] * (env_scale * live_at(t))
        e0_s[:, at] = e
        put(0, e)
        for m in range(1, 9):
            put(m, e * y[m])
        acc[...] += scatter(t)
        return carry

    def phase_b(t, carry):
        at = span(t)
        big_g[:, at] = dot(cat[...], hot_t[:, at])
        g0 = big_g[chan(0), at]
        t1 = big_g[chan(1), at] * harm[1:2, at]
        for m in range(2, 4):
            t1 = t1 + big_g[chan(m), at] * harm[m : m + 1, at]
        t2 = big_g[chan(4), at] * harm[4:5, at]
        for m in range(5, 9):
            t2 = t2 + big_g[chan(m), at] * harm[m : m + 1, at]
        t1_s[:, at] = t1
        t2_s[:, at] = t2
        v = v_s[:, at]
        pre = latent(0, xh_s[:, at], xl_s[:, at], [v * g0, v * t1, v * t2])
        sg = sigmoid(pre)
        x = x_s[:, at] + pre * sg
        d1_s[:, at] = sg * (1.0 + pre * (1.0 - sg))
        xh, xl = halves(x)
        x_s[:, at] = x
        xh_s[:, at] = xh
        xl_s[:, at] = xl
        ge = dot(w_ge[...], jnp.concatenate([xh, xl, xh], 0))
        g_s[:, at] = ge[0:C]
        e = ge[C:] * (env_scale * live_at(t))
        e1_s[:, at] = e
        put(0, e)
        for m in range(1, 9):
            put(m, e * harm[m : m + 1, at])
        acc[...] += scatter(t)
        return carry

    def path(i):
        return w_path[:, i : i + 1]

    def phase_c(t, carry):
        at = span(t)
        big_h[:, at] = dot(cat[...], hot_t[:, at])

        def sums(low, high):
            a = big_g[chan(low), at] * big_h[chan(low), at]
            b = big_h[chan(low), at] * harm[low : low + 1, at]
            for m in range(low + 1, high):
                h = big_h[chan(m), at]
                a = a + big_g[chan(m), at] * h
                b = b + h * harm[m : m + 1, at]
            return a, b

        a1, b1 = sums(1, 4)
        a2, b2 = sums(4, 9)
        g0 = big_g[chan(0), at]
        h0 = big_h[chan(0), at]
        c0 = path(0) * g0 + path(1) * t1_s[:, at] + path(2) * t2_s[:, at]
        h4 = path(4) * g0
        h6 = path(6) * g0
        p0 = c0 * h0
        p1 = path(3) * a1 + h4 * b1
        p2 = path(5) * a2 + h6 * b2
        v = v_s[:, at]
        g = g_s[:, at]
        gv = g * v
        pre = latent(1, xh_s[:, at], xl_s[:, at], [gv * p0, gv * p1, gv * p2])
        sg = sigmoid(pre)
        x = x_s[:, at] + pre * sg
        d2 = sg * (1.0 + pre * (1.0 - sg))
        hid = dot(w_fin[...], stacked(x))
        sg = sigmoid(hid)
        live = live_at(t)
        ow = w_out[:, 0:1]
        eps_s[:, at] = jnp.sum(fold(ow * (hid * sg)), 0, keepdims=True) * live
        dhid = (ow * live) * (sg * (1.0 + hid * (1.0 - sg)))
        dx = dot(w_finb[...], stacked(dhid))
        dm = dot(w_latb[1], stacked(dx * d2))
        dx_s[:, at] = dx + dm[0:C]
        ds0, ds1, ds2 = dm[chan(1)], dm[chan(2)], dm[chan(3)]
        dgv = ds0 * p0 + ds1 * p1 + ds2 * p2
        dg_s[:, at] = dgv * v
        dv_s[:, at] = dgv * g
        u0 = ds0 * gv
        u1 = ds1 * gv
        u2 = ds2 * gv
        k1 = u1 * path(3)
        k2 = u2 * path(5)
        j1 = u1 * h4
        j2 = u2 * h6
        k1_s[:, at] = k1
        k2_s[:, at] = k2
        j1_s[:, at] = j1
        j2_s[:, at] = j2
        uh = u0 * h0
        dg0_s[:, at] = uh * path(0) + u1 * path(4) * b1 + u2 * path(6) * b2
        dt1_s[:, at] = uh * path(1)
        dt2_s[:, at] = uh * path(2)
        put(0, u0 * c0)
        for m in range(1, 9):
            k, j = (k1, j1) if m < 4 else (k2, j2)
            put(m, k * big_g[chan(m), at] + j * harm[m : m + 1, at])
        acc[...] += scatter(t)
        return carry

    def phase_d(t, carry):
        at = span(t)
        work[...] = dot(cat[...], hot_t[:, at])
        de = work[chan(0), :]
        for m in range(1, 9):
            de = de + work[chan(m), :] * harm[m : m + 1, at]
        de = de * (env_scale * live_at(t))
        deh, del_ = halves(de)
        dgh, dgl = halves(dg_s[:, at])
        dx = dx_s[:, at] + dot(
            w_b1[...], jnp.concatenate([deh, dgh, del_, dgl, deh, dgh], 0)
        )
        dm = dot(w_latb[0], stacked(dx * d1_s[:, at]))
        dx_s[:, at] = dx + dm[0:C]
        ds0, ds1, ds2 = dm[chan(1)], dm[chan(2)], dm[chan(3)]
        v = v_s[:, at]
        dv_s[:, at] += ds0 * big_g[chan(0), at] + ds1 * t1_s[:, at] + ds2 * t2_s[:, at]
        dt1 = dt1_s[:, at] + ds1 * v
        dt2 = dt2_s[:, at] + ds2 * v
        put(0, dg0_s[:, at] + ds0 * v)
        e = e1_s[:, at]
        for m in range(1, 9):
            if m < 4:
                k, j, dt = k1_s[:, at], j1_s[:, at], dt1
            else:
                k, j, dt = k2_s[:, at], j2_s[:, at], dt2
            h = big_h[chan(m), at]
            dy_s[8 * m : 8 * m + 8, at] = fold(
                j * h + dt * big_g[chan(m), at] + e * work[chan(m), :]
            )
            put(m, k * h + dt * harm[m : m + 1, at])
        acc[...] += scatter(t)
        return carry

    def phase_e(t, carry):
        at = span(t)
        work[...] = dot(cat[...], hot_t[:, at])
        de = work[chan(0), :]
        for m in range(1, 9):
            de = de + work[chan(m), :] * harm[m : m + 1, at]
        de = de * (env_scale * live_at(t))
        e = e0_s[:, at]
        dy = [None]
        for m in range(1, 9):
            part = dy_s[8 * m : 8 * m + 8, at] + fold(e * work[chan(m), :])
            dy.append(jnp.sum(part, 0, keepdims=True))
        deh, del_ = halves(de)
        dvh, dvl = halves(dv_s[:, at])
        dx = dx_s[:, at] + dot(
            w_b0[...], jnp.concatenate([deh, dvh, del_, dvl, deh, dvh], 0)
        )
        dbasis = dot(w_embb[...], stacked(dx * d0_s[:, at]))
        drho = -jnp.sum(dbasis * basis_s[:, at], 0, keepdims=True)
        u = geo[0:3, at]
        rho = geo[3:4, at]
        inv = 1.0 / rho
        ux, uy, uz = u[0:1], u[1:2], u[2:3]
        dux = dy[1] + root_three * (uy * dy[4] + uz * dy[6] + ux * dy[7]) - ux * dy[8]
        duy = dy[2] + root_three * (ux * dy[4] + uz * dy[5] - uy * dy[7]) - uy * dy[8]
        duz = dy[3] + root_three * (uy * dy[5] + ux * dy[6]) + 2.0 * (uz * dy[8])
        along = drho - (dux * ux + duy * uy + duz * uz) * inv
        dd = [dux * inv + ux * along, duy * inv + uy * along, duz * inv + uz * along]
        rows = jnp.concatenate(dd + [eps_s[:, at]], 0)
        first = hi(rows)
        rest = rows - first
        second = hi(rest)
        acc_own[...] += dot(
            jnp.concatenate([first, second, rest - second, jnp.zeros((4, T), f32)], 0).astype(bf16),
            hot[at, :],
        )
        s = slot_s[:, at]
        spread = jnp.concatenate([s * dd[c] for c in range(3)], 0)
        first = hi(spread)
        acc_near[...] += dot_nt(
            jnp.concatenate([first, spread - first], 0).astype(bf16), near[:, at]
        )
        return carry

    acc[...] = jnp.zeros(acc.shape, f32)
    lax.fori_loop(0, steps, phase_a, 0)
    for phase in (phase_b, phase_c, phase_d):
        make_cat()
        acc[...] = jnp.zeros(acc.shape, f32)
        lax.fori_loop(0, steps, phase, 0)
    make_cat()
    acc_own[...] = jnp.zeros(acc_own.shape, f32)
    acc_near[...] = jnp.zeros(acc_near.shape, f32)
    lax.fori_loop(0, steps, phase_e, 0)

    own = acc_own[0:4, :] + acc_own[4:8, :] + acc_own[8:12, :]
    site_ref[...] = own[3:4, :]
    ghosts = acc_near[0:96, :] + acc_near[96:192, :]
    for c in range(3):
        local = jnp.concatenate([ghosts[c * 32 : c * 32 + 1], ghosts[c * 32 + 1 : c * 32 + 2]], 1)
        own_ref[c : c + 1, :] = local - own[c : c + 1]
    ghost_ref[...] = jnp.zeros(ghost_ref.shape, f32)
    for k in range(27):
        for c in range(3):
            ghost_ref[k, c : c + 1, :] = ghosts[c * 32 + k + 2 : c * 32 + k + 3, :]


def pair_grads(table, positions, features, center, nbr, count, params):
    pairs = center.shape[1]
    atoms = positions.shape[1]
    T = TILE

    def wide(rows, dtype=f32):
        return pltpu.VMEM((rows, pairs), dtype)

    scratch = [
        pltpu.VMEM((128, 144), bf16),
        pltpu.VMEM((128, 192), bf16),
        pltpu.VMEM((128, 192), bf16),
        pltpu.VMEM((64, 192), bf16),
        pltpu.VMEM((64, 192), bf16),
        pltpu.VMEM((2, 128, 256), bf16),
        pltpu.VMEM((2, 256, 192), bf16),
        pltpu.VMEM((64, 384), bf16),
        pltpu.VMEM((64, 384), bf16),
        pltpu.VMEM((8, 192), bf16),
        pltpu.VMEM((64, 8), f32),
        pltpu.VMEM((64, 8), f32),
        pltpu.VMEM((29 * 64, 128), bf16),
        pltpu.VMEM((96, 128), f32),
        pltpu.VMEM((288, 128), bf16),
        pltpu.VMEM((80, atoms), bf16),
        pltpu.VMEM((pairs, atoms), bf16),
        wide(2 * atoms, bf16),
        wide(128, bf16),
        wide(32),
        wide(8),
        wide(16),
        wide(8),
        wide(64),
        wide(64, bf16),
        wide(64, bf16),
    ]
    scratch += [wide(64)] * 18
    scratch[-1] = wide(64)
    scratch += [wide(72), wide(1)]
    scratch += [
        wide(576),
        wide(576),
        pltpu.VMEM((576, T), f32),
        pltpu.VMEM((576, T), bf16),
        pltpu.VMEM((576, T), bf16),
        pltpu.VMEM((576, atoms), f32),
        pltpu.VMEM((576, 2 * atoms), bf16),
        pltpu.VMEM((16, atoms), f32),
        pltpu.VMEM((192, 128), f32),
    ]
    vmem = pl.BlockSpec(memory_space=pltpu.VMEM)
    return pl.pallas_call(
        pair_kernel,
        out_shape=(
            jax.ShapeDtypeStruct((1, atoms), f32),
            jax.ShapeDtypeStruct((3, atoms), f32),
            jax.ShapeDtypeStruct((27, 8, 128), f32),
        ),
        in_specs=[vmem] * 14,
        out_specs=(vmem, vmem, vmem),
        scratch_shapes=scratch,
        compiler_params=pltpu.CompilerParams(vmem_limit_bytes=60 * 1024 * 1024),
        cost_estimate=pl.CostEstimate(flops=40 * 10**9, bytes_accessed=10**6, transcendentals=10**6),
    )(table, positions, features, center, nbr, count, *params)


def local(
    positions, features, ghost_rows, pair_center, pair_nbr, pair_count,
    emb_weight, value_weight, env_weight, path_weight, latent_weight, gate_weight,
    final_weight, out_weight,
):
    rows = ghost_rows.reshape(1, -1)
    table = halo(positions, features, rows)
    site, own, ghost = pair_grads(
        table, positions, features,
        pair_center.reshape(1, -1), pair_nbr.reshape(1, -1), pair_count.reshape(1, 1),
        (emb_weight, value_weight, env_weight, path_weight, latent_weight, gate_weight,
         final_weight, out_weight.reshape(1, -1)),
    )
    forces = give_back(ghost, own, rows)
    return (site.reshape(-1), forces)


def solution(mesh):
    placed = (
        P(None, axes),
        P(None, axes),
        P(axes),
        P(axes),
        P(axes),
        P(axes),
    ) + (P(),) * 8
    return jax.shard_map(
        local,
        mesh=mesh,
        in_specs=placed,
        out_specs=(P(axes), P(None, axes)),
        check_vma=False,
    )
```

```python
import functools

import jax
import jax.numpy as jnp
from jax import lax
from jax.experimental import pallas as pl
from jax.experimental.pallas import tpu as pltpu
from jax.sharding import PartitionSpec as P

edge_length = 3.0
env_scale = 0.125
root_three = 1.7320508075688772
axes = ("gx", "gy", "gz")
MESH = pl.DeviceIdType.MESH
f32 = jnp.float32
bf16 = jnp.bfloat16
C = 64
SLOTS = [k for k in range(27) if k != 13]
ROWS = 72
TILE = 256
SKEW = 1
GROUP = 3
RING = 6


def offset(k):
    return (k // 9 - 1, k // 3 % 3 - 1, k % 3 - 1)


def peer(k, sign):
    me = [lax.axis_index(a) for a in axes]
    sizes = [lax.axis_size(a) for a in axes]
    return tuple(lax.rem(m + sign * o + s, s) for m, o, s in zip(me, offset(k), sizes))


def greet():
    barrier = pltpu.get_barrier_semaphore()
    for k in SLOTS:
        pl.semaphore_signal(barrier, inc=1, device_id=peer(k, 1), device_id_type=MESH)
    pl.semaphore_wait(barrier, len(SLOTS))


def dot(a, b):
    return jnp.dot(a, b, preferred_element_type=f32)


def dot_nt(a, b):
    return lax.dot_general(a, b, (((1,), (1,)), ((), ())), preferred_element_type=f32)


def hi(x):
    return x.astype(bf16).astype(f32)


def halves(x):
    first = x.astype(bf16)
    return first, (x - first.astype(f32)).astype(bf16)


def thirds(x):
    first = hi(x)
    rest = x - first
    second = hi(rest)
    return first, second, rest - second


def halo_kernel(pos_ref, feat_ref, rows_ref, out_ref, send_buf, send_sem, recv_sem):
    greet()
    atoms = feat_ref.shape[1]
    sent = rows_ref.shape[1]
    pick = (
        lax.broadcasted_iota(jnp.int32, (atoms, sent), 0)
        == jnp.broadcast_to(rows_ref[...], (atoms, sent))
    ).astype(bf16)
    send_buf[0:C, :] = dot(feat_ref[...], pick)
    parts = thirds(pos_ref[...])
    send_buf[C : C + 3, :] = (
        dot(parts[0].astype(bf16), pick)
        + dot(parts[1].astype(bf16), pick)
        + dot(parts[2].astype(bf16), pick)
    )
    send_buf[C + 3 : ROWS, :] = jnp.zeros((ROWS - C - 3, sent), f32)
    copies = []
    for k in SLOTS:
        copy = pltpu.make_async_remote_copy(
            src_ref=send_buf,
            dst_ref=out_ref.at[k],
            send_sem=send_sem.at[k],
            recv_sem=recv_sem.at[k],
            device_id=peer(k, -1),
            device_id_type=MESH,
        )
        copy.start()
        copies.append(copy)
    out_ref[13] = jnp.zeros((ROWS, sent), f32)
    for copy in copies:
        copy.wait()


def halo(positions, features, rows):
    sent = rows.shape[1]
    return pl.pallas_call(
        halo_kernel,
        out_shape=jax.ShapeDtypeStruct((27, ROWS, sent), f32),
        in_specs=[pl.BlockSpec(memory_space=pltpu.VMEM)] * 3,
        out_specs=pl.BlockSpec(memory_space=pltpu.VMEM),
        scratch_shapes=[
            pltpu.VMEM((ROWS, sent), f32),
            pltpu.SemaphoreType.DMA((27,)),
            pltpu.SemaphoreType.DMA((27,)),
        ],
        compiler_params=pltpu.CompilerParams(collective_id=0, has_side_effects=True),
    )(positions, features, rows)


def return_kernel(ghost_ref, own_ref, rows_ref, force_ref, landed, send_sem, recv_sem):
    greet()
    copies = []
    for k in SLOTS:
        copy = pltpu.make_async_remote_copy(
            src_ref=ghost_ref.at[k],
            dst_ref=landed.at[k],
            send_sem=send_sem.at[k],
            recv_sem=recv_sem.at[k],
            device_id=peer(k, 1),
            device_id_type=MESH,
        )
        copy.start()
        copies.append(copy)
    atoms = own_ref.shape[1]
    sent = rows_ref.shape[1]
    pick = (
        lax.broadcasted_iota(jnp.int32, (atoms, sent), 0)
        == jnp.broadcast_to(rows_ref[...], (atoms, sent))
    ).astype(bf16)
    for copy in copies:
        copy.wait()
    owned = landed[SLOTS[0]]
    for k in SLOTS[1:]:
        owned = owned + landed[k]
    parts = thirds(owned)
    back = (
        dot_nt(parts[0].astype(bf16), pick)
        + dot_nt(parts[1].astype(bf16), pick)
        + dot_nt(parts[2].astype(bf16), pick)
    )
    force_ref[...] = -(own_ref[...] + back[0:3, :])


def give_back(ghost_grad, own_grad, rows):
    sent = rows.shape[1]
    return pl.pallas_call(
        return_kernel,
        out_shape=jax.ShapeDtypeStruct(own_grad.shape, f32),
        in_specs=[pl.BlockSpec(memory_space=pltpu.VMEM)] * 3,
        out_specs=pl.BlockSpec(memory_space=pltpu.VMEM),
        scratch_shapes=[
            pltpu.VMEM((27, 8, sent), f32),
            pltpu.SemaphoreType.DMA((27,)),
            pltpu.SemaphoreType.DMA((27,)),
        ],
        compiler_params=pltpu.CompilerParams(collective_id=1, has_side_effects=True),
    )(ghost_grad, own_grad, rows)


def forward_stack(weight):
    first = hi(weight)
    return jnp.concatenate([first, first, weight - first], 0).T.astype(bf16)


def backward_stack(weight):
    first = hi(weight)
    return jnp.concatenate([first, first, weight - first], 1).astype(bf16)


def stacked(x):
    first, second = halves(x)
    return jnp.concatenate([first, second, first], 0)


def sigmoid(x):
    return 0.5 * jnp.tanh(0.5 * x) + 0.5


def fold(x):
    total = x[0:8]
    for i in range(1, C // 8):
        total = total + x[8 * i : 8 * i + 8]
    return total


def chan(m):
    return slice(m * C, (m + 1) * C)


def pair_kernel(
    table_ref, pos_ref, feat_ref, center_ref, nbr_ref, count_ref,
    emb_ref, value_ref, env_ref, path_ref, latent_ref, gate_ref, final_ref, out_ref,
    site_ref, own_ref, ghost_ref,
    w_emb, w_ve, w_ge, w_fin, w_finb, w_lat, w_latb, w_b1, w_b0, w_embb, w_path, w_out,
    tab_feat, tab_pos, tab_pos3, tab_own,
    hot, hot_t, near, slot_s, geo, harm, basis_s,
    x_s, xh_s, xl_s, d0_s, d1_s, v_s, g_s, e0_s, e1_s, t1_s, t2_s,
    dx_s, dv_s, dg_s, dg0_s, dt1_s, dt2_s, k1_s, k2_s, j1_s, j2_s, dy_s, eps_s,
    big_g, big_h, work, msg_h, msg_l, acc, cat, acc_own, acc_near,
):
    pairs = center_ref.shape[1]
    atoms = pos_ref.shape[1]
    T = TILE
    steps = pairs // T

    stage = pl.program_id(0)

    @pl.when(stage == 0)
    def _():
        emb = emb_ref[...]
        emb_h = hi(emb)
        emb_l = emb - emb_h
        w_emb[...] = jnp.concatenate(
            [
                jnp.concatenate([emb_h, emb_h[2 * C :]], 0),
                jnp.concatenate([emb_l, jnp.zeros((8, C), f32)], 0),
            ],
            1,
        ).T.astype(bf16)
        low_h = emb_h[2 * C :]
        w_embb[...] = jnp.concatenate(
            [
                jnp.concatenate([low_h, low_h], 1),
                jnp.concatenate([emb_l[2 * C :], jnp.zeros((8, C), f32)], 1),
            ],
            0,
        ).astype(bf16)
        w_ve[...] = forward_stack(jnp.concatenate([value_ref[...], env_ref[0]], 1))
        w_ge[...] = forward_stack(jnp.concatenate([gate_ref[0], env_ref[1]], 1))
        w_b0[...] = backward_stack(jnp.concatenate([env_ref[0], value_ref[...]], 1))
        w_b1[...] = backward_stack(jnp.concatenate([env_ref[1], gate_ref[0]], 1))
        w_fin[...] = forward_stack(final_ref[...])
        w_finb[...] = backward_stack(final_ref[...])
        w_out[...] = jnp.broadcast_to(out_ref[...], (8, C)).T
        for layer in range(2):
            cols = jnp.concatenate([path_ref[layer], jnp.ones((1, C), f32)], 0).T
            if layer == 0:
                w_path[...] = cols
            scaled = jnp.concatenate(
                [latent_ref[layer, 0:C]]
                + [latent_ref[layer, chan(i + 1)] * cols[:, i : i + 1] for i in range(3)],
                0,
            )
            first = hi(scaled)
            w_lat[layer] = jnp.concatenate([first, scaled - first], 1).T.astype(bf16)
            w_latb[layer] = backward_stack(scaled)

        tab_pos[...] = jnp.zeros(tab_pos.shape, f32)
        tab_feat[0:C, :] = feat_ref[...]
        tab_feat[14 * C : 15 * C, 128:256] = jnp.zeros((C, 128), bf16)
        for k in range(27):
            half = slice(k % 2 * 128, k % 2 * 128 + 128)
            at = 1 + k // 2
            tab_feat[chan(at), half] = table_ref[k, 0:C, :].astype(bf16)
            for c in range(3):
                tab_pos[c * 16 + at : c * 16 + at + 1, half] = (
                    table_ref[k, C + c : C + c + 1, :] + edge_length * offset(k)[c]
                )
        for c in range(3):
            tab_pos[c * 16 : c * 16 + 1, :] = pos_ref[c : c + 1, :]
        for i, part in enumerate(thirds(tab_pos[...])):
            tab_pos3[i * 48 : (i + 1) * 48, :] = part.astype(bf16)
        tab_own[0:C, :] = feat_ref[...]
        tab_own[C : C + 16, :] = jnp.concatenate(
            list(thirds(pos_ref[...])) + [jnp.zeros((7, atoms), f32)], 0
        ).astype(bf16)

    def span(t):
        return slice(t * T, (t + 1) * T)

    def live_at(t):
        at = lax.broadcasted_iota(jnp.int32, (1, T), 1) + t * T
        return jnp.where(at < jnp.broadcast_to(count_ref[...], (1, T)), 1.0, 0.0)

    def scatter(t):
        many = GROUP
        if t % many == many - 1:
            at = slice((t + 1 - many) * T, (t + 1) * T)
            late = t % RING
            held = slice((late + 1 - many) * T, (late + 1) * T)
            add = dot(msg_h[:, held], hot[at, :]) + dot(msg_l[:, held], hot[at, :])
            if t == many - 1:
                acc[...] = add
            else:
                acc[...] += add

    def gather(t):
        return dot(cat[...], hot_t[:, span(t)])

    def put(m, t, x):
        first, second = halves(x)
        msg_h[chan(m), span(t % RING)] = first
        msg_l[chan(m), span(t % RING)] = second

    def make_cat():
        first, second = halves(acc[...])
        cat[:, 0:atoms] = first
        cat[:, atoms : 2 * atoms] = second

    def spread_latent(xh, xl, scalars):
        split = [halves(s) for s in scalars]
        high = jnp.concatenate([xh] + [s[0] for s in split], 0)
        low = jnp.concatenate([xl] + [s[1] for s in split], 0)
        return high, low

    def latent(layer, high, low):
        both = dot(w_lat[layer], high)
        return both[0:C] + both[C:] + dot(w_lat[layer, 0:C], low)

    def run(phase):
        gens = [phase(t) for t in range(steps)]
        done = 0
        tick = 0
        alive = [True] * steps
        while any(alive):
            for t in range(steps):
                if alive[t] and tick >= t * SKEW:
                    try:
                        next(gens[t])
                    except StopIteration:
                        alive[t] = False
            tick += 1

    def row(m, at):
        return harm[m : m + 1, at]

    def phase_a(t):
        at = span(t)
        nbr = nbr_ref[:, at]
        rest = jnp.bitwise_and(nbr, 255)
        slot = jnp.right_shift(nbr, 8)
        r = (
            lax.broadcasted_iota(jnp.int32, (256, T), 0) == jnp.broadcast_to(rest, (256, T))
        ).astype(bf16)
        near[:, at] = r
        s = jnp.where(
            lax.broadcasted_iota(jnp.int32, (16, T), 0) == jnp.broadcast_to(slot, (16, T)), 1.0, 0.0
        )
        slot_s[:, at] = s
        own = (
            lax.broadcasted_iota(jnp.int32, (atoms, T), 0)
            == jnp.broadcast_to(center_ref[:, at], (atoms, T))
        ).astype(f32)
        hot_t[0:atoms, at] = own.astype(bf16)
        hot_t[atoms : 2 * atoms, at] = own.astype(bf16)
        hot[at, :] = own.T.astype(bf16)
        yield
        found = dot(tab_own[...], hot_t[0:atoms, at])
        far = dot(tab_pos3[...], near[:, at])
        yield
        pos_i = found[C : C + 3] + found[C + 3 : C + 6] + found[C + 6 : C + 9]
        far = far[0:48] + far[48:96] + far[96:144]
        pos_j = jnp.concatenate(
            [jnp.sum(far[c * 16 : c * 16 + 16] * s, 0, keepdims=True) for c in range(3)], 0
        )
        feat_i = found[0:C].astype(bf16)
        feat_j = jnp.zeros((C, T), f32)
        for k0 in range(0, 15, 5):
            got = dot(tab_feat[k0 * C : (k0 + 5) * C, :], near[:, at])
            for k in range(5):
                feat_j = feat_j + got[chan(k)] * s[k0 + k : k0 + k + 1]
        yield
        d = pos_j - pos_i
        rho = jnp.sqrt(jnp.sum(d * d, 0, keepdims=True) + 1.0)
        inv = 1.0 / rho
        u = d * inv
        ux, uy, uz = u[0:1], u[1:2], u[2:3]
        y = [
            None, ux, uy, uz,
            root_three * ux * uy,
            root_three * uy * uz,
            root_three * uz * ux,
            (root_three * 0.5) * (ux * ux - uy * uy),
            0.5 * (2.0 * uz * uz - ux * ux - uy * uy),
        ]
        for m in range(1, 9):
            harm[m : m + 1, at] = y[m]
        geo[0:3, at] = u
        geo[3:4, at] = rho
        mu = lax.broadcasted_iota(jnp.int32, (8, T), 0).astype(f32) * 1.25
        z = rho - mu
        basis = jnp.exp(-0.5 * z * z)
        basis_s[:, at] = basis * z
        joined = jnp.concatenate(
            [
                feat_i,
                feat_j.astype(bf16),
                jnp.concatenate([basis, basis - hi(basis)], 0).astype(bf16),
            ],
            0,
        )
        yield
        pre = dot(w_emb[...], joined)
        yield
        pre = pre[0:C] + pre[C:]
        sg = sigmoid(pre)
        x = pre * sg
        d0_s[:, at] = sg * (1.0 + pre * (1.0 - sg))
        xh, xl = halves(x)
        x_s[:, at] = x
        xh_s[:, at] = xh
        xl_s[:, at] = xl
        yield
        ve = dot(w_ve[...], jnp.concatenate([xh, xl, xh], 0))
        yield
        v_s[:, at] = ve[0:C]
        e = ve[C:] * (env_scale * live_at(t))
        e0_s[:, at] = e
        put(0, t, e)
        for m in range(1, 9):
            put(m, t, e * row(m, at))
        yield
        scatter(t)

    def phase_b(t):
        at = span(t)
        big_g[:, at] = gather(t)
        yield
        g0 = big_g[chan(0), at]
        t1 = big_g[chan(1), at] * row(1, at)
        for m in range(2, 4):
            t1 = t1 + big_g[chan(m), at] * row(m, at)
        t2 = big_g[chan(4), at] * row(4, at)
        for m in range(5, 9):
            t2 = t2 + big_g[chan(m), at] * row(m, at)
        t1_s[:, at] = t1
        t2_s[:, at] = t2
        v = v_s[:, at]
        high, low = spread_latent(xh_s[:, at], xl_s[:, at], [v * g0, v * t1, v * t2])
        yield
        pre = latent(0, high, low)
        yield
        sg = sigmoid(pre)
        x = x_s[:, at] + pre * sg
        d1_s[:, at] = sg * (1.0 + pre * (1.0 - sg))
        xh, xl = halves(x)
        x_s[:, at] = x
        xh_s[:, at] = xh
        xl_s[:, at] = xl
        yield
        ge = dot(w_ge[...], jnp.concatenate([xh, xl, xh], 0))
        yield
        g_s[:, at] = ge[0:C]
        e = ge[C:] * (env_scale * live_at(t))
        e1_s[:, at] = e
        put(0, t, e)
        for m in range(1, 9):
            put(m, t, e * row(m, at))
        yield
        scatter(t)

    def path(i):
        return w_path[:, i : i + 1]

    def phase_c(t):
        at = span(t)
        big_h[:, at] = gather(t)
        yield

        def sums(low, high):
            a = big_g[chan(low), at] * big_h[chan(low), at]
            b = big_h[chan(low), at] * row(low, at)
            for m in range(low + 1, high):
                h = big_h[chan(m), at]
                a = a + big_g[chan(m), at] * h
                b = b + h * row(m, at)
            return a, b

        a1, b1 = sums(1, 4)
        a2, b2 = sums(4, 9)
        g0 = big_g[chan(0), at]
        c0 = path(0) * g0 + path(1) * t1_s[:, at] + path(2) * t2_s[:, at]
        h4 = path(4) * g0
        h6 = path(6) * g0
        p0 = c0 * big_h[chan(0), at]
        p1 = path(3) * a1 + h4 * b1
        p2 = path(5) * a2 + h6 * b2
        gv = g_s[:, at] * v_s[:, at]
        high, low = spread_latent(xh_s[:, at], xl_s[:, at], [gv * p0, gv * p1, gv * p2])
        yield
        pre = latent(1, high, low)
        yield
        sg = sigmoid(pre)
        x = x_s[:, at] + pre * sg
        d2 = sg * (1.0 + pre * (1.0 - sg))
        x = stacked(x)
        yield
        hid = dot(w_fin[...], x)
        yield
        sg = sigmoid(hid)
        live = live_at(t)
        ow = w_out[:, 0:1]
        eps_s[:, at] = jnp.sum(fold(ow * (hid * sg)), 0, keepdims=True) * live
        dhid = (ow * live) * (sg * (1.0 + hid * (1.0 - sg)))
        dhid = stacked(dhid)
        yield
        dx = dot(w_finb[...], dhid)
        yield
        dpre = stacked(dx * d2)
        yield
        dm = dot(w_latb[1], dpre)
        yield
        dx_s[:, at] = dx + dm[0:C]
        ds0, ds1, ds2 = dm[chan(1)], dm[chan(2)], dm[chan(3)]
        dgv = ds0 * p0 + ds1 * p1 + ds2 * p2
        v = v_s[:, at]
        g = g_s[:, at]
        dg_s[:, at] = dgv * v
        dv_s[:, at] = dgv * g
        u0 = ds0 * gv
        u1 = ds1 * gv
        u2 = ds2 * gv
        k1 = u1 * path(3)
        k2 = u2 * path(5)
        j1 = u1 * h4
        j2 = u2 * h6
        k1_s[:, at] = k1
        k2_s[:, at] = k2
        j1_s[:, at] = j1
        j2_s[:, at] = j2
        uh = u0 * big_h[chan(0), at]
        dg0_s[:, at] = uh * path(0) + u1 * path(4) * b1 + u2 * path(6) * b2
        dt1_s[:, at] = uh * path(1)
        dt2_s[:, at] = uh * path(2)
        put(0, t, u0 * c0)
        for m in range(1, 9):
            k, j = (k1, j1) if m < 4 else (k2, j2)
            put(m, t, k * big_g[chan(m), at] + j * row(m, at))
        yield
        scatter(t)

    def phase_d(t):
        at = span(t)
        wat = span(t % RING)
        work[:, wat] = gather(t)
        yield
        de = work[chan(0), wat]
        for m in range(1, 9):
            de = de + work[chan(m), wat] * row(m, at)
        de = de * (env_scale * live_at(t))
        deh, del_ = halves(de)
        dgh, dgl = halves(dg_s[:, at])
        pair = jnp.concatenate([deh, dgh, del_, dgl, deh, dgh], 0)
        yield
        dx = dot(w_b1[...], pair)
        yield
        dx = dx_s[:, at] + dx
        dpre = stacked(dx * d1_s[:, at])
        yield
        dm = dot(w_latb[0], dpre)
        yield
        dx_s[:, at] = dx + dm[0:C]
        ds0, ds1, ds2 = dm[chan(1)], dm[chan(2)], dm[chan(3)]
        v = v_s[:, at]
        dv_s[:, at] += ds0 * big_g[chan(0), at] + ds1 * t1_s[:, at] + ds2 * t2_s[:, at]
        dt1 = dt1_s[:, at] + ds1 * v
        dt2 = dt2_s[:, at] + ds2 * v
        put(0, t, dg0_s[:, at] + ds0 * v)
        e = e1_s[:, at]
        for m in range(1, 9):
            if m < 4:
                k, j, dt = k1_s[:, at], j1_s[:, at], dt1
            else:
                k, j, dt = k2_s[:, at], j2_s[:, at], dt2
            h = big_h[chan(m), at]
            dy_s[8 * m : 8 * m + 8, at] = fold(
                j * h + dt * big_g[chan(m), at] + e * work[chan(m), wat]
            )
            put(m, t, k * h + dt * row(m, at))
        yield
        scatter(t)

    def phase_e(t):
        at = span(t)
        wat = span(t % RING)
        work[:, wat] = gather(t)
        yield
        de = work[chan(0), wat]
        for m in range(1, 9):
            de = de + work[chan(m), wat] * row(m, at)
        de = de * (env_scale * live_at(t))
        deh, del_ = halves(de)
        dvh, dvl = halves(dv_s[:, at])
        pair = jnp.concatenate([deh, dvh, del_, dvl, deh, dvh], 0)
        e = e0_s[:, at]
        dy = [None]
        for m in range(1, 9):
            part = dy_s[8 * m : 8 * m + 8, at] + fold(e * work[chan(m), wat])
            dy.append(jnp.sum(part, 0, keepdims=True))
        yield
        dx = dot(w_b0[...], pair)
        yield
        dpre = jnp.concatenate(halves((dx_s[:, at] + dx) * d0_s[:, at]), 0)
        yield
        dbasis = dot(w_embb[...], dpre)
        dbasis = dbasis[0:8] + dbasis[8:16]
        yield
        drho = -jnp.sum(dbasis * basis_s[:, at], 0, keepdims=True)
        u = geo[0:3, at]
        rho = geo[3:4, at]
        inv = 1.0 / rho
        ux, uy, uz = u[0:1], u[1:2], u[2:3]
        dux = dy[1] + root_three * (uy * dy[4] + uz * dy[6] + ux * dy[7]) - ux * dy[8]
        duy = dy[2] + root_three * (ux * dy[4] + uz * dy[5] - uy * dy[7]) - uy * dy[8]
        duz = dy[3] + root_three * (uy * dy[5] + ux * dy[6]) + 2.0 * (uz * dy[8])
        along = drho - (dux * ux + duy * uy + duz * uz) * inv
        dd = [dux * inv + ux * along, duy * inv + uy * along, duz * inv + uz * along]
        rows = jnp.concatenate(dd + [eps_s[:, at]], 0)
        first = hi(rows)
        rest = rows - first
        second = hi(rest)
        rows = jnp.concatenate(
            [first, second, rest - second, jnp.zeros((4, T), f32)], 0
        ).astype(bf16)
        s = slot_s[:, at]
        spread = jnp.concatenate([s * dd[c] for c in range(3)], 0)
        first = hi(spread)
        spread = jnp.concatenate([first, spread - first], 0).astype(bf16)
        yield
        acc_own[...] += dot(rows, hot[at, :])
        acc_near[...] += dot_nt(spread, near[:, at])

    @pl.when(stage == 0)
    def _():
        run(phase_a)
        make_cat()

    for number, phase in ((1, phase_b), (2, phase_c), (3, phase_d)):

        @pl.when(stage == number)
        def _(phase=phase):
            run(phase)
            make_cat()

    @pl.when(stage == 4)
    def _():
        acc_own[...] = jnp.zeros(acc_own.shape, f32)
        acc_near[...] = jnp.zeros(acc_near.shape, f32)
        run(phase_e)
        own = acc_own[0:4, :] + acc_own[4:8, :] + acc_own[8:12, :]
        site_ref[...] = own[3:4, :]
        ghosts = acc_near[0:48, :] + acc_near[48:96, :]
        for c in range(3):
            own_ref[c : c + 1, :] = ghosts[c * 16 : c * 16 + 1] - own[c : c + 1]
        ghost_ref[...] = jnp.zeros(ghost_ref.shape, f32)
        for k in range(27):
            half = slice(k % 2 * 128, k % 2 * 128 + 128)
            for c in range(3):
                at = c * 16 + 1 + k // 2
                ghost_ref[k, c : c + 1, :] = ghosts[at : at + 1, half]


def pair_grads(table, positions, features, center, nbr, count, params):
    pairs = center.shape[1]
    atoms = positions.shape[1]
    T = TILE

    def wide(rows, dtype=f32):
        return pltpu.VMEM((rows, pairs), dtype)

    scratch = [
        pltpu.VMEM((128, 144), bf16),
        pltpu.VMEM((128, 192), bf16),
        pltpu.VMEM((128, 192), bf16),
        pltpu.VMEM((64, 192), bf16),
        pltpu.VMEM((64, 192), bf16),
        pltpu.VMEM((2, 128, 256), bf16),
        pltpu.VMEM((2, 256, 192), bf16),
        pltpu.VMEM((64, 384), bf16),
        pltpu.VMEM((64, 384), bf16),
        pltpu.VMEM((16, 128), bf16),
        pltpu.VMEM((64, 8), f32),
        pltpu.VMEM((64, 8), f32),
        pltpu.VMEM((15 * 64, 256), bf16),
        pltpu.VMEM((48, 256), f32),
        pltpu.VMEM((144, 256), bf16),
        pltpu.VMEM((80, atoms), bf16),
        pltpu.VMEM((pairs, atoms), bf16),
        wide(2 * atoms, bf16),
        wide(256, bf16),
        wide(16),
        wide(8),
        wide(16),
        wide(8),
        wide(64),
        wide(64, bf16),
        wide(64, bf16),
    ]
    scratch += [wide(64)] * 18
    scratch += [wide(72), wide(1)]
    scratch += [
        wide(576),
        wide(576),
        pltpu.VMEM((576, RING * T), f32),
        pltpu.VMEM((576, RING * T), bf16),
        pltpu.VMEM((576, RING * T), bf16),
        pltpu.VMEM((576, atoms), f32),
        pltpu.VMEM((576, 2 * atoms), bf16),
        pltpu.VMEM((16, atoms), f32),
        pltpu.VMEM((96, 256), f32),
    ]
    vmem = pl.BlockSpec(memory_space=pltpu.VMEM)
    return pl.pallas_call(
        pair_kernel,
        out_shape=(
            jax.ShapeDtypeStruct((1, atoms), f32),
            jax.ShapeDtypeStruct((3, atoms), f32),
            jax.ShapeDtypeStruct((27, 8, 128), f32),
        ),
        grid=(5,),
        in_specs=[vmem] * 14,
        out_specs=(vmem, vmem, vmem),
        scratch_shapes=scratch,
        compiler_params=pltpu.CompilerParams(vmem_limit_bytes=60 * 1024 * 1024),
        cost_estimate=pl.CostEstimate(flops=40 * 10**9, bytes_accessed=10**6, transcendentals=10**6),
    )(table, positions, features, center, nbr, count, *params)


def local(
    positions, features, ghost_rows, pair_center, pair_nbr, pair_count,
    emb_weight, value_weight, env_weight, path_weight, latent_weight, gate_weight,
    final_weight, out_weight,
):
    rows = ghost_rows.reshape(1, -1)
    table = halo(positions, features, rows)
    site, own, ghost = pair_grads(
        table, positions, features,
        pair_center.reshape(1, -1), pair_nbr.reshape(1, -1), pair_count.reshape(1, 1),
        (emb_weight, value_weight, env_weight, path_weight, latent_weight, gate_weight,
         final_weight, out_weight.reshape(1, -1)),
    )
    forces = give_back(ghost, own, rows)
    return (site.reshape(-1), forces)


def solution(mesh):
    placed = (
        P(None, axes),
        P(None, axes),
        P(axes),
        P(axes),
        P(axes),
        P(axes),
    ) + (P(),) * 8
    return jax.shard_map(
        local,
        mesh=mesh,
        in_specs=placed,
        out_specs=(P(axes), P(None, axes)),
        check_vma=False,
    )
```

```python
import functools

import jax
import jax.numpy as jnp
from jax import lax
from jax.experimental import pallas as pl
from jax.experimental.pallas import tpu as pltpu
from jax.sharding import PartitionSpec as P

edge_length = 3.0
env_scale = 0.125
root_three = 1.7320508075688772
axes = ("gx", "gy", "gz")
MESH = pl.DeviceIdType.MESH
f32 = jnp.float32
bf16 = jnp.bfloat16
C = 64
PLANE = [10, 12, 14, 16, 9, 11, 15, 17]
NEAR = PLANE + [4, 22]
ROWS = 72
TILE = 256
SKEW = 1
GROUP = 3
RING = 6


def offset(k):
    return (k // 9 - 1, k // 3 % 3 - 1, k % 3 - 1)


def peer(k, sign):
    me = [lax.axis_index(a) for a in axes]
    sizes = [lax.axis_size(a) for a in axes]
    return tuple(lax.rem(m + sign * o + s, s) for m, o, s in zip(me, offset(k), sizes))


def greet():
    barrier = pltpu.get_barrier_semaphore()
    for k in NEAR:
        pl.semaphore_signal(barrier, inc=1, device_id=peer(k, 1), device_id_type=MESH)
    pl.semaphore_wait(barrier, len(NEAR))


def dot(a, b):
    return jnp.dot(a, b, preferred_element_type=f32)


def dot_nt(a, b):
    return lax.dot_general(a, b, (((1,), (1,)), ((), ())), preferred_element_type=f32)


def hi(x):
    return x.astype(bf16).astype(f32)


def halves(x):
    first = x.astype(bf16)
    return first, (x - first.astype(f32)).astype(bf16)


def thirds(x):
    first = hi(x)
    rest = x - first
    second = hi(rest)
    return first, second, rest - second


def halo_kernel(pos_ref, feat_ref, rows_ref, out_ref, send_buf, send_sem, recv_sem):
    greet()
    atoms = feat_ref.shape[1]
    sent = rows_ref.shape[1]
    pick = (
        lax.broadcasted_iota(jnp.int32, (atoms, sent), 0)
        == jnp.broadcast_to(rows_ref[...], (atoms, sent))
    ).astype(bf16)
    send_buf[0:C, :] = dot(feat_ref[...], pick)
    parts = thirds(pos_ref[...])
    send_buf[C : C + 3, :] = (
        dot(parts[0].astype(bf16), pick)
        + dot(parts[1].astype(bf16), pick)
        + dot(parts[2].astype(bf16), pick)
    )
    send_buf[C + 3 : ROWS, :] = jnp.zeros((ROWS - C - 3, sent), f32)
    def send(source, k, to):
        copy = pltpu.make_async_remote_copy(
            src_ref=source,
            dst_ref=out_ref.at[k],
            send_sem=send_sem.at[k],
            recv_sem=recv_sem.at[k],
            device_id=peer(to, -1),
            device_id_type=MESH,
        )
        copy.start()
        return copy

    plane = [send(send_buf, k, k) for k in PLANE]
    later = [send(send_buf, k, k) for k in (4, 22)]
    out_ref[13] = jnp.zeros((ROWS, sent), f32)
    for k, copy in zip(PLANE, plane):
        copy.wait_recv()
        later.append(send(out_ref.at[k], k - 9, 4))
        later.append(send(out_ref.at[k], k + 9, 22))
    for copy in plane:
        copy.wait_send()
    for copy in later:
        copy.wait()


def halo(positions, features, rows):
    sent = rows.shape[1]
    return pl.pallas_call(
        halo_kernel,
        out_shape=jax.ShapeDtypeStruct((27, ROWS, sent), f32),
        in_specs=[pl.BlockSpec(memory_space=pltpu.VMEM)] * 3,
        out_specs=pl.BlockSpec(memory_space=pltpu.VMEM),
        scratch_shapes=[
            pltpu.VMEM((ROWS, sent), f32),
            pltpu.SemaphoreType.DMA((27,)),
            pltpu.SemaphoreType.DMA((27,)),
        ],
        compiler_params=pltpu.CompilerParams(collective_id=0, has_side_effects=True),
    )(positions, features, rows)


def return_kernel(ghost_ref, own_ref, rows_ref, force_ref, sides, plane, landed, send_sem, recv_sem):
    greet()

    def send(source, target, k, to):
        copy = pltpu.make_async_remote_copy(
            src_ref=source,
            dst_ref=target,
            send_sem=send_sem.at[k],
            recv_sem=recv_sem.at[k],
            device_id=peer(to, 1),
            device_id_type=MESH,
        )
        copy.start()
        return copy

    first = [
        send(ghost_ref.at[0:9], sides.at[0], 4, 4),
        send(ghost_ref.at[18:27], sides.at[1], 22, 22),
    ]
    atoms = own_ref.shape[1]
    sent = rows_ref.shape[1]
    pick = (
        lax.broadcasted_iota(jnp.int32, (atoms, sent), 0)
        == jnp.broadcast_to(rows_ref[...], (atoms, sent))
    ).astype(bf16)
    for copy in first:
        copy.wait()
    plane[...] = ghost_ref[9:18] + sides[0] + sides[1]
    second = [send(plane.at[k - 9], landed.at[k - 9], k, k) for k in PLANE]
    owned = plane[4]
    for copy in second:
        copy.wait()
    for k in PLANE:
        owned = owned + landed[k - 9]
    parts = thirds(owned)
    back = (
        dot_nt(parts[0].astype(bf16), pick)
        + dot_nt(parts[1].astype(bf16), pick)
        + dot_nt(parts[2].astype(bf16), pick)
    )
    force_ref[...] = -(own_ref[...] + back[0:3, :])


def give_back(ghost_grad, own_grad, rows):
    sent = rows.shape[1]
    return pl.pallas_call(
        return_kernel,
        out_shape=jax.ShapeDtypeStruct(own_grad.shape, f32),
        in_specs=[pl.BlockSpec(memory_space=pltpu.VMEM)] * 3,
        out_specs=pl.BlockSpec(memory_space=pltpu.VMEM),
        scratch_shapes=[
            pltpu.VMEM((2, 9, 8, sent), f32),
            pltpu.VMEM((9, 8, sent), f32),
            pltpu.VMEM((9, 8, sent), f32),
            pltpu.SemaphoreType.DMA((27,)),
            pltpu.SemaphoreType.DMA((27,)),
        ],
        compiler_params=pltpu.CompilerParams(collective_id=1, has_side_effects=True),
    )(ghost_grad, own_grad, rows)


def forward_stack(weight):
    first = hi(weight)
    return jnp.concatenate([first, first, weight - first], 0).T.astype(bf16)


def backward_stack(weight):
    first = hi(weight)
    return jnp.concatenate([first, first, weight - first], 1).astype(bf16)


def stacked(x):
    first, second = halves(x)
    return jnp.concatenate([first, second, first], 0)


def sigmoid(x):
    return 0.5 * jnp.tanh(0.5 * x) + 0.5


def fold(x):
    total = x[0:8]
    for i in range(1, C // 8):
        total = total + x[8 * i : 8 * i + 8]
    return total


def chan(m):
    return slice(m * C, (m + 1) * C)


def pair_kernel(
    table_ref, pos_ref, feat_ref, center_ref, nbr_ref, count_ref,
    emb_ref, value_ref, env_ref, path_ref, latent_ref, gate_ref, final_ref, out_ref,
    site_ref, own_ref, ghost_ref,
    w_emb, w_ve, w_ge, w_fin, w_finb, w_lat, w_latb, w_b1, w_b0, w_embb, w_path, w_out,
    tab_feat, tab_pos, tab_pos3, tab_own,
    hot, hot_t, near, slot_s, geo, harm, basis_s,
    x_s, xh_s, xl_s, d0_s, d1_s, v_s, g_s, e0_s, e1_s, t1_s, t2_s,
    dx_s, dv_s, dg_s, dg0_s, dt1_s, dt2_s, k1_s, k2_s, j1_s, j2_s, dy_s, eps_s,
    big_g, big_h, work, msg_h, msg_l, acc, cat, acc_own, acc_near,
):
    pairs = center_ref.shape[1]
    atoms = pos_ref.shape[1]
    T = TILE
    steps = pairs // T

    stage = pl.program_id(0)

    @pl.when(stage == 0)
    def _():
        emb = emb_ref[...].T
        emb_h = hi(emb)
        emb_l = emb - emb_h
        w_emb[...] = jnp.concatenate(
            [
                jnp.concatenate([emb_h, emb_h[2 * C :]], 0),
                jnp.concatenate([emb_l, jnp.zeros((8, C), f32)], 0),
            ],
            1,
        ).T.astype(bf16)
        low_h = emb_h[2 * C :]
        w_embb[...] = jnp.concatenate(
            [
                jnp.concatenate([low_h, low_h], 1),
                jnp.concatenate([emb_l[2 * C :], jnp.zeros((8, C), f32)], 1),
            ],
            0,
        ).astype(bf16)
        w_ve[...] = forward_stack(jnp.concatenate([value_ref[...], env_ref[0]], 1))
        w_ge[...] = forward_stack(jnp.concatenate([gate_ref[0], env_ref[1]], 1))
        w_b0[...] = backward_stack(jnp.concatenate([env_ref[0], value_ref[...]], 1))
        w_b1[...] = backward_stack(jnp.concatenate([env_ref[1], gate_ref[0]], 1))
        w_fin[...] = forward_stack(final_ref[...])
        w_finb[...] = backward_stack(final_ref[...])
        w_out[...] = jnp.broadcast_to(out_ref[...], (8, C)).T
        for layer in range(2):
            cols = jnp.concatenate([path_ref[:, layer], jnp.ones((1, C), f32)], 0).T
            if layer == 0:
                w_path[...] = cols
            mix = latent_ref[layer].T
            scaled = jnp.concatenate(
                [mix[0:C]] + [mix[chan(i + 1)] * cols[:, i : i + 1] for i in range(3)],
                0,
            )
            first = hi(scaled)
            w_lat[layer] = jnp.concatenate([first, scaled - first], 1).T.astype(bf16)
            w_latb[layer] = backward_stack(scaled)

        tab_pos[...] = jnp.zeros(tab_pos.shape, f32)
        tab_feat[0:C, :] = feat_ref[...]
        tab_feat[14 * C : 15 * C, 128:256] = jnp.zeros((C, 128), bf16)
        for k in range(27):
            half = slice(k % 2 * 128, k % 2 * 128 + 128)
            at = 1 + k // 2
            tab_feat[chan(at), half] = table_ref[k, 0:C, :].astype(bf16)
            for c in range(3):
                tab_pos[c * 16 + at : c * 16 + at + 1, half] = (
                    table_ref[k, C + c : C + c + 1, :] + edge_length * offset(k)[c]
                )
        for c in range(3):
            tab_pos[c * 16 : c * 16 + 1, :] = pos_ref[c : c + 1, :]
        for i, part in enumerate(thirds(tab_pos[...])):
            tab_pos3[i * 48 : (i + 1) * 48, :] = part.astype(bf16)
        tab_own[0:C, :] = feat_ref[...]
        tab_own[C : C + 16, :] = jnp.concatenate(
            list(thirds(pos_ref[...])) + [jnp.zeros((7, atoms), f32)], 0
        ).astype(bf16)

    def span(t):
        return slice(t * T, (t + 1) * T)

    def live_at(t):
        at = lax.broadcasted_iota(jnp.int32, (1, T), 1) + t * T
        return jnp.where(at < jnp.broadcast_to(count_ref[...], (1, T)), 1.0, 0.0)

    def scatter(t):
        many = GROUP
        if t % many == many - 1:
            at = slice((t + 1 - many) * T, (t + 1) * T)
            late = t % RING
            held = slice((late + 1 - many) * T, (late + 1) * T)
            add = dot(msg_h[:, held], hot[at, :]) + dot(msg_l[:, held], hot[at, :])
            if t == many - 1:
                acc[...] = add
            else:
                acc[...] += add

    def gather(t):
        return dot(cat[...], hot_t[:, span(t)])

    def put(m, t, x):
        first, second = halves(x)
        msg_h[chan(m), span(t % RING)] = first
        msg_l[chan(m), span(t % RING)] = second

    def make_cat():
        first, second = halves(acc[...])
        cat[:, 0:atoms] = first
        cat[:, atoms : 2 * atoms] = second

    def spread_latent(xh, xl, scalars):
        split = [halves(s) for s in scalars]
        high = jnp.concatenate([xh] + [s[0] for s in split], 0)
        low = jnp.concatenate([xl] + [s[1] for s in split], 0)
        return high, low

    def latent(layer, high, low):
        both = dot(w_lat[layer], high)
        return both[0:C] + both[C:] + dot(w_lat[layer, 0:C], low)

    def run(phase):
        gens = [phase(t) for t in range(steps)]
        done = 0
        tick = 0
        alive = [True] * steps
        while any(alive):
            for t in range(steps):
                if alive[t] and tick >= t * SKEW:
                    try:
                        next(gens[t])
                    except StopIteration:
                        alive[t] = False
            tick += 1

    def row(m, at):
        return harm[m : m + 1, at]

    def phase_a(t):
        at = span(t)
        nbr = nbr_ref[:, at]
        rest = jnp.bitwise_and(nbr, 255)
        slot = jnp.right_shift(nbr, 8)
        r = (
            lax.broadcasted_iota(jnp.int32, (256, T), 0) == jnp.broadcast_to(rest, (256, T))
        ).astype(bf16)
        near[:, at] = r
        s = jnp.where(
            lax.broadcasted_iota(jnp.int32, (16, T), 0) == jnp.broadcast_to(slot, (16, T)), 1.0, 0.0
        )
        slot_s[:, at] = s
        own = (
            lax.broadcasted_iota(jnp.int32, (atoms, T), 0)
            == jnp.broadcast_to(center_ref[:, at], (atoms, T))
        ).astype(f32)
        hot_t[0:atoms, at] = own.astype(bf16)
        hot_t[atoms : 2 * atoms, at] = own.astype(bf16)
        hot[at, :] = own.T.astype(bf16)
        yield
        found = dot(tab_own[...], hot_t[0:atoms, at])
        far = dot(tab_pos3[...], near[:, at])
        yield
        pos_i = found[C : C + 3] + found[C + 3 : C + 6] + found[C + 6 : C + 9]
        far = far[0:48] + far[48:96] + far[96:144]
        pos_j = jnp.concatenate(
            [jnp.sum(far[c * 16 : c * 16 + 16] * s, 0, keepdims=True) for c in range(3)], 0
        )
        feat_i = found[0:C].astype(bf16)
        feat_j = jnp.zeros((C, T), f32)
        for k0 in range(0, 15, 5):
            got = dot(tab_feat[k0 * C : (k0 + 5) * C, :], near[:, at])
            for k in range(5):
                feat_j = feat_j + got[chan(k)] * s[k0 + k : k0 + k + 1]
        yield
        d = pos_j - pos_i
        rho = jnp.sqrt(jnp.sum(d * d, 0, keepdims=True) + 1.0)
        inv = 1.0 / rho
        u = d * inv
        ux, uy, uz = u[0:1], u[1:2], u[2:3]
        y = [
            None, ux, uy, uz,
            root_three * ux * uy,
            root_three * uy * uz,
            root_three * uz * ux,
            (root_three * 0.5) * (ux * ux - uy * uy),
            0.5 * (2.0 * uz * uz - ux * ux - uy * uy),
        ]
        for m in range(1, 9):
            harm[m : m + 1, at] = y[m]
        geo[0:3, at] = u
        geo[3:4, at] = rho
        mu = lax.broadcasted_iota(jnp.int32, (8, T), 0).astype(f32) * 1.25
        z = rho - mu
        basis = jnp.exp(-0.5 * z * z)
        basis_s[:, at] = basis * z
        joined = jnp.concatenate(
            [
                feat_i,
                feat_j.astype(bf16),
                jnp.concatenate([basis, basis - hi(basis)], 0).astype(bf16),
            ],
            0,
        )
        yield
        pre = dot(w_emb[...], joined)
        yield
        pre = pre[0:C] + pre[C:]
        sg = sigmoid(pre)
        x = pre * sg
        d0_s[:, at] = sg * (1.0 + pre * (1.0 - sg))
        xh, xl = halves(x)
        x_s[:, at] = x
        xh_s[:, at] = xh
        xl_s[:, at] = xl
        yield
        ve = dot(w_ve[...], jnp.concatenate([xh, xl, xh], 0))
        yield
        v_s[:, at] = ve[0:C]
        e = ve[C:] * (env_scale * live_at(t))
        e0_s[:, at] = e
        put(0, t, e)
        for m in range(1, 9):
            put(m, t, e * row(m, at))
        yield
        scatter(t)

    def phase_b(t):
        at = span(t)
        big_g[:, at] = gather(t)
        yield
        g0 = big_g[chan(0), at]
        t1 = big_g[chan(1), at] * row(1, at)
        for m in range(2, 4):
            t1 = t1 + big_g[chan(m), at] * row(m, at)
        t2 = big_g[chan(4), at] * row(4, at)
        for m in range(5, 9):
            t2 = t2 + big_g[chan(m), at] * row(m, at)
        t1_s[:, at] = t1
        t2_s[:, at] = t2
        v = v_s[:, at]
        high, low = spread_latent(xh_s[:, at], xl_s[:, at], [v * g0, v * t1, v * t2])
        yield
        pre = latent(0, high, low)
        yield
        sg = sigmoid(pre)
        x = x_s[:, at] + pre * sg
        d1_s[:, at] = sg * (1.0 + pre * (1.0 - sg))
        xh, xl = halves(x)
        x_s[:, at] = x
        xh_s[:, at] = xh
        xl_s[:, at] = xl
        yield
        ge = dot(w_ge[...], jnp.concatenate([xh, xl, xh], 0))
        yield
        g_s[:, at] = ge[0:C]
        e = ge[C:] * (env_scale * live_at(t))
        e1_s[:, at] = e
        put(0, t, e)
        for m in range(1, 9):
            put(m, t, e * row(m, at))
        yield
        scatter(t)

    def path(i):
        return w_path[:, i : i + 1]

    def phase_c(t):
        at = span(t)
        big_h[:, at] = gather(t)
        yield

        def sums(low, high):
            a = big_g[chan(low), at] * big_h[chan(low), at]
            b = big_h[chan(low), at] * row(low, at)
            for m in range(low + 1, high):
                h = big_h[chan(m), at]
                a = a + big_g[chan(m), at] * h
                b = b + h * row(m, at)
            return a, b

        a1, b1 = sums(1, 4)
        a2, b2 = sums(4, 9)
        g0 = big_g[chan(0), at]
        c0 = path(0) * g0 + path(1) * t1_s[:, at] + path(2) * t2_s[:, at]
        h4 = path(4) * g0
        h6 = path(6) * g0
        p0 = c0 * big_h[chan(0), at]
        p1 = path(3) * a1 + h4 * b1
        p2 = path(5) * a2 + h6 * b2
        gv = g_s[:, at] * v_s[:, at]
        high, low = spread_latent(xh_s[:, at], xl_s[:, at], [gv * p0, gv * p1, gv * p2])
        yield
        pre = latent(1, high, low)
        yield
        sg = sigmoid(pre)
        x = x_s[:, at] + pre * sg
        d2 = sg * (1.0 + pre * (1.0 - sg))
        x = stacked(x)
        yield
        hid = dot(w_fin[...], x)
        yield
        sg = sigmoid(hid)
        live = live_at(t)
        ow = w_out[:, 0:1]
        eps_s[:, at] = jnp.sum(fold(ow * (hid * sg)), 0, keepdims=True) * live
        dhid = (ow * live) * (sg * (1.0 + hid * (1.0 - sg)))
        dhid = stacked(dhid)
        yield
        dx = dot(w_finb[...], dhid)
        yield
        dpre = stacked(dx * d2)
        yield
        dm = dot(w_latb[1], dpre)
        yield
        dx_s[:, at] = dx + dm[0:C]
        ds0, ds1, ds2 = dm[chan(1)], dm[chan(2)], dm[chan(3)]
        dgv = ds0 * p0 + ds1 * p1 + ds2 * p2
        v = v_s[:, at]
        g = g_s[:, at]
        dg_s[:, at] = dgv * v
        dv_s[:, at] = dgv * g
        u0 = ds0 * gv
        u1 = ds1 * gv
        u2 = ds2 * gv
        k1 = u1 * path(3)
        k2 = u2 * path(5)
        j1 = u1 * h4
        j2 = u2 * h6
        k1_s[:, at] = k1
        k2_s[:, at] = k2
        j1_s[:, at] = j1
        j2_s[:, at] = j2
        uh = u0 * big_h[chan(0), at]
        dg0_s[:, at] = uh * path(0) + u1 * path(4) * b1 + u2 * path(6) * b2
        dt1_s[:, at] = uh * path(1)
        dt2_s[:, at] = uh * path(2)
        put(0, t, u0 * c0)
        for m in range(1, 9):
            k, j = (k1, j1) if m < 4 else (k2, j2)
            put(m, t, k * big_g[chan(m), at] + j * row(m, at))
        yield
        scatter(t)

    def phase_d(t):
        at = span(t)
        wat = span(t % RING)
        work[:, wat] = gather(t)
        yield
        de = work[chan(0), wat]
        for m in range(1, 9):
            de = de + work[chan(m), wat] * row(m, at)
        de = de * (env_scale * live_at(t))
        deh, del_ = halves(de)
        dgh, dgl = halves(dg_s[:, at])
        pair = jnp.concatenate([deh, dgh, del_, dgl, deh, dgh], 0)
        yield
        dx = dot(w_b1[...], pair)
        yield
        dx = dx_s[:, at] + dx
        dpre = stacked(dx * d1_s[:, at])
        yield
        dm = dot(w_latb[0], dpre)
        yield
        dx_s[:, at] = dx + dm[0:C]
        ds0, ds1, ds2 = dm[chan(1)], dm[chan(2)], dm[chan(3)]
        v = v_s[:, at]
        dv_s[:, at] += ds0 * big_g[chan(0), at] + ds1 * t1_s[:, at] + ds2 * t2_s[:, at]
        dt1 = dt1_s[:, at] + ds1 * v
        dt2 = dt2_s[:, at] + ds2 * v
        put(0, t, dg0_s[:, at] + ds0 * v)
        e = e1_s[:, at]
        for m in range(1, 9):
            if m < 4:
                k, j, dt = k1_s[:, at], j1_s[:, at], dt1
            else:
                k, j, dt = k2_s[:, at], j2_s[:, at], dt2
            h = big_h[chan(m), at]
            dy_s[8 * m : 8 * m + 8, at] = fold(
                j * h + dt * big_g[chan(m), at] + e * work[chan(m), wat]
            )
            put(m, t, k * h + dt * row(m, at))
        yield
        scatter(t)

    def phase_e(t):
        at = span(t)
        wat = span(t % RING)
        work[:, wat] = gather(t)
        yield
        de = work[chan(0), wat]
        for m in range(1, 9):
            de = de + work[chan(m), wat] * row(m, at)
        de = de * (env_scale * live_at(t))
        deh, del_ = halves(de)
        dvh, dvl = halves(dv_s[:, at])
        pair = jnp.concatenate([deh, dvh, del_, dvl, deh, dvh], 0)
        e = e0_s[:, at]
        dy = [None]
        for m in range(1, 9):
            part = dy_s[8 * m : 8 * m + 8, at] + fold(e * work[chan(m), wat])
            dy.append(jnp.sum(part, 0, keepdims=True))
        yield
        dx = dot(w_b0[...], pair)
        yield
        dpre = jnp.concatenate(halves((dx_s[:, at] + dx) * d0_s[:, at]), 0)
        yield
        dbasis = dot(w_embb[...], dpre)
        dbasis = dbasis[0:8] + dbasis[8:16]
        yield
        drho = -jnp.sum(dbasis * basis_s[:, at], 0, keepdims=True)
        u = geo[0:3, at]
        rho = geo[3:4, at]
        inv = 1.0 / rho
        ux, uy, uz = u[0:1], u[1:2], u[2:3]
        dux = dy[1] + root_three * (uy * dy[4] + uz * dy[6] + ux * dy[7]) - ux * dy[8]
        duy = dy[2] + root_three * (ux * dy[4] + uz * dy[5] - uy * dy[7]) - uy * dy[8]
        duz = dy[3] + root_three * (uy * dy[5] + ux * dy[6]) + 2.0 * (uz * dy[8])
        along = drho - (dux * ux + duy * uy + duz * uz) * inv
        dd = [dux * inv + ux * along, duy * inv + uy * along, duz * inv + uz * along]
        rows = jnp.concatenate(dd + [eps_s[:, at]], 0)
        first = hi(rows)
        rest = rows - first
        second = hi(rest)
        rows = jnp.concatenate(
            [first, second, rest - second, jnp.zeros((4, T), f32)], 0
        ).astype(bf16)
        s = slot_s[:, at]
        spread = jnp.concatenate([s * dd[c] for c in range(3)], 0)
        first = hi(spread)
        spread = jnp.concatenate([first, spread - first], 0).astype(bf16)
        yield
        acc_own[...] += dot(rows, hot[at, :])
        acc_near[...] += dot_nt(spread, near[:, at])

    @pl.when(stage == 0)
    def _():
        run(phase_a)
        make_cat()

    for number, phase in ((1, phase_b), (2, phase_c), (3, phase_d)):

        @pl.when(stage == number)
        def _(phase=phase):
            run(phase)
            make_cat()

    @pl.when(stage == 4)
    def _():
        acc_own[...] = jnp.zeros(acc_own.shape, f32)
        acc_near[...] = jnp.zeros(acc_near.shape, f32)
        run(phase_e)
        own = acc_own[0:4, :] + acc_own[4:8, :] + acc_own[8:12, :]
        site_ref[...] = own[3:4, :]
        ghosts = acc_near[0:48, :] + acc_near[48:96, :]
        for c in range(3):
            own_ref[c : c + 1, :] = ghosts[c * 16 : c * 16 + 1] - own[c : c + 1]
        ghost_ref[...] = jnp.zeros(ghost_ref.shape, f32)
        for k in range(27):
            half = slice(k % 2 * 128, k % 2 * 128 + 128)
            for c in range(3):
                at = c * 16 + 1 + k // 2
                ghost_ref[k, c : c + 1, :] = ghosts[at : at + 1, half]


def pair_grads(table, positions, features, center, nbr, count, params):
    pairs = center.shape[1]
    atoms = positions.shape[1]
    T = TILE
    emb, value, env, path, latent, *rest = params
    params = (emb.T, value, env, path.transpose(1, 0, 2), latent.transpose(0, 2, 1), *rest)

    def wide(rows, dtype=f32):
        return pltpu.VMEM((rows, pairs), dtype)

    scratch = [
        pltpu.VMEM((128, 144), bf16),
        pltpu.VMEM((128, 192), bf16),
        pltpu.VMEM((128, 192), bf16),
        pltpu.VMEM((64, 192), bf16),
        pltpu.VMEM((64, 192), bf16),
        pltpu.VMEM((2, 128, 256), bf16),
        pltpu.VMEM((2, 256, 192), bf16),
        pltpu.VMEM((64, 384), bf16),
        pltpu.VMEM((64, 384), bf16),
        pltpu.VMEM((16, 128), bf16),
        pltpu.VMEM((64, 8), f32),
        pltpu.VMEM((64, 8), f32),
        pltpu.VMEM((15 * 64, 256), bf16),
        pltpu.VMEM((48, 256), f32),
        pltpu.VMEM((144, 256), bf16),
        pltpu.VMEM((80, atoms), bf16),
        pltpu.VMEM((pairs, atoms), bf16),
        wide(2 * atoms, bf16),
        wide(256, bf16),
        wide(16),
        wide(8),
        wide(16),
        wide(8),
        wide(64),
        wide(64, bf16),
        wide(64, bf16),
    ]
    scratch += [wide(64)] * 18
    scratch += [wide(72), wide(1)]
    scratch += [
        wide(576),
        wide(576),
        pltpu.VMEM((576, RING * T), f32),
        pltpu.VMEM((576, RING * T), bf16),
        pltpu.VMEM((576, RING * T), bf16),
        pltpu.VMEM((576, atoms), f32),
        pltpu.VMEM((576, 2 * atoms), bf16),
        pltpu.VMEM((16, atoms), f32),
        pltpu.VMEM((96, 256), f32),
    ]
    vmem = pl.BlockSpec(memory_space=pltpu.VMEM)
    return pl.pallas_call(
        pair_kernel,
        out_shape=(
            jax.ShapeDtypeStruct((1, atoms), f32),
            jax.ShapeDtypeStruct((3, atoms), f32),
            jax.ShapeDtypeStruct((27, 8, 128), f32),
        ),
        grid=(5,),
        in_specs=[vmem] * 14,
        out_specs=(vmem, vmem, vmem),
        scratch_shapes=scratch,
        compiler_params=pltpu.CompilerParams(vmem_limit_bytes=60 * 1024 * 1024),
        cost_estimate=pl.CostEstimate(flops=40 * 10**9, bytes_accessed=10**6, transcendentals=10**6),
    )(table, positions, features, center, nbr, count, *params)


def local(
    positions, features, ghost_rows, pair_center, pair_nbr, pair_count,
    emb_weight, value_weight, env_weight, path_weight, latent_weight, gate_weight,
    final_weight, out_weight,
):
    rows = ghost_rows.reshape(1, -1)
    table = halo(positions, features, rows)
    site, own, ghost = pair_grads(
        table, positions, features,
        pair_center.reshape(1, -1), pair_nbr.reshape(1, -1), pair_count.reshape(1, 1),
        (emb_weight, value_weight, env_weight, path_weight, latent_weight, gate_weight,
         final_weight, out_weight.reshape(1, -1)),
    )
    forces = give_back(ghost, own, rows)
    return (site.reshape(-1), forces)


def solution(mesh):
    placed = (
        P(None, axes),
        P(None, axes),
        P(axes),
        P(axes),
        P(axes),
        P(axes),
    ) + (P(),) * 8
    return jax.shard_map(
        local,
        mesh=mesh,
        in_specs=placed,
        out_specs=(P(axes), P(None, axes)),
        check_vma=False,
    )
```

```python
import functools

import jax
import jax.numpy as jnp
from jax import lax
from jax.experimental import pallas as pl
from jax.experimental.pallas import tpu as pltpu
from jax.sharding import PartitionSpec as P

edge_length = 3.0
env_scale = 0.125
root_three = 1.7320508075688772
axes = ("gx", "gy", "gz")
MESH = pl.DeviceIdType.MESH
f32 = jnp.float32
bf16 = jnp.bfloat16
C = 64
PLANE = [10, 12, 14, 16, 9, 11, 15, 17]
NEAR = PLANE + [4, 22]
ROWS = 72
TILE = 256
SKEW = 1
GROUP = 2
RING = 6


def offset(k):
    return (k // 9 - 1, k // 3 % 3 - 1, k % 3 - 1)


def peer(k, sign):
    me = [lax.axis_index(a) for a in axes]
    sizes = [lax.axis_size(a) for a in axes]
    return tuple(lax.rem(m + sign * o + s, s) for m, o, s in zip(me, offset(k), sizes))


def greet():
    barrier = pltpu.get_barrier_semaphore()
    for k in NEAR:
        pl.semaphore_signal(barrier, inc=1, device_id=peer(k, 1), device_id_type=MESH)
    pl.semaphore_wait(barrier, len(NEAR))


def dot(a, b):
    return jnp.dot(a, b, preferred_element_type=f32)


def dot_nt(a, b):
    return lax.dot_general(a, b, (((1,), (1,)), ((), ())), preferred_element_type=f32)


def hi(x):
    return x.astype(bf16).astype(f32)


def halves(x):
    first = x.astype(bf16)
    return first, (x - first.astype(f32)).astype(bf16)


def thirds(x):
    first = hi(x)
    rest = x - first
    second = hi(rest)
    return first, second, rest - second


def halo_kernel(pos_ref, feat_ref, rows_ref, out_ref, send_buf, send_sem, recv_sem):
    greet()
    atoms = feat_ref.shape[1]
    sent = rows_ref.shape[1]
    pick = (
        lax.broadcasted_iota(jnp.int32, (atoms, sent), 0)
        == jnp.broadcast_to(rows_ref[...], (atoms, sent))
    ).astype(bf16)
    send_buf[0:C, :] = dot(feat_ref[...], pick)
    parts = thirds(pos_ref[...])
    send_buf[C : C + 3, :] = (
        dot(parts[0].astype(bf16), pick)
        + dot(parts[1].astype(bf16), pick)
        + dot(parts[2].astype(bf16), pick)
    )
    send_buf[C + 3 : ROWS, :] = jnp.zeros((ROWS - C - 3, sent), f32)
    def send(source, k, to):
        copy = pltpu.make_async_remote_copy(
            src_ref=source,
            dst_ref=out_ref.at[k],
            send_sem=send_sem.at[k],
            recv_sem=recv_sem.at[k],
            device_id=peer(to, -1),
            device_id_type=MESH,
        )
        copy.start()
        return copy

    plane = [send(send_buf, k, k) for k in PLANE]
    later = [send(send_buf, k, k) for k in (4, 22)]
    out_ref[13] = jnp.zeros((ROWS, sent), f32)
    for k, copy in zip(PLANE, plane):
        copy.wait_recv()
        later.append(send(out_ref.at[k], k - 9, 4))
        later.append(send(out_ref.at[k], k + 9, 22))
    for copy in plane:
        copy.wait_send()
    for copy in later:
        copy.wait()


def halo(positions, features, rows):
    sent = rows.shape[1]
    return pl.pallas_call(
        halo_kernel,
        out_shape=jax.ShapeDtypeStruct((27, ROWS, sent), f32),
        in_specs=[pl.BlockSpec(memory_space=pltpu.VMEM)] * 3,
        out_specs=pl.BlockSpec(memory_space=pltpu.VMEM),
        scratch_shapes=[
            pltpu.VMEM((ROWS, sent), f32),
            pltpu.SemaphoreType.DMA((27,)),
            pltpu.SemaphoreType.DMA((27,)),
        ],
        compiler_params=pltpu.CompilerParams(collective_id=0, has_side_effects=True),
    )(positions, features, rows)


def return_kernel(ghost_ref, own_ref, rows_ref, force_ref, sides, plane, landed, send_sem, recv_sem):
    greet()

    def send(source, target, k, to):
        copy = pltpu.make_async_remote_copy(
            src_ref=source,
            dst_ref=target,
            send_sem=send_sem.at[k],
            recv_sem=recv_sem.at[k],
            device_id=peer(to, 1),
            device_id_type=MESH,
        )
        copy.start()
        return copy

    first = [
        send(ghost_ref.at[0:9], sides.at[0], 4, 4),
        send(ghost_ref.at[18:27], sides.at[1], 22, 22),
    ]
    atoms = own_ref.shape[1]
    sent = rows_ref.shape[1]
    pick = (
        lax.broadcasted_iota(jnp.int32, (atoms, sent), 0)
        == jnp.broadcast_to(rows_ref[...], (atoms, sent))
    ).astype(bf16)
    for copy in first:
        copy.wait()
    plane[...] = ghost_ref[9:18] + sides[0] + sides[1]
    second = [send(plane.at[k - 9], landed.at[k - 9], k, k) for k in PLANE]
    owned = plane[4]
    for copy in second:
        copy.wait()
    for k in PLANE:
        owned = owned + landed[k - 9]
    parts = thirds(owned)
    back = (
        dot_nt(parts[0].astype(bf16), pick)
        + dot_nt(parts[1].astype(bf16), pick)
        + dot_nt(parts[2].astype(bf16), pick)
    )
    force_ref[...] = -(own_ref[...] + back[0:3, :])


def give_back(ghost_grad, own_grad, rows):
    sent = rows.shape[1]
    return pl.pallas_call(
        return_kernel,
        out_shape=jax.ShapeDtypeStruct(own_grad.shape, f32),
        in_specs=[pl.BlockSpec(memory_space=pltpu.VMEM)] * 3,
        out_specs=pl.BlockSpec(memory_space=pltpu.VMEM),
        scratch_shapes=[
            pltpu.VMEM((2, 9, 8, sent), f32),
            pltpu.VMEM((9, 8, sent), f32),
            pltpu.VMEM((9, 8, sent), f32),
            pltpu.SemaphoreType.DMA((27,)),
            pltpu.SemaphoreType.DMA((27,)),
        ],
        compiler_params=pltpu.CompilerParams(collective_id=1, has_side_effects=True),
    )(ghost_grad, own_grad, rows)


def forward_stack(weight):
    first = hi(weight)
    return jnp.concatenate([first, first, weight - first], 0).T.astype(bf16)


def backward_stack(weight):
    first = hi(weight)
    return jnp.concatenate([first, first, weight - first], 1).astype(bf16)


def stacked(x):
    first, second = halves(x)
    return jnp.concatenate([first, second, first], 0)


def sigmoid(x):
    return 0.5 * jnp.tanh(0.5 * x) + 0.5


def fold(x):
    total = x[0:8]
    for i in range(1, C // 8):
        total = total + x[8 * i : 8 * i + 8]
    return total


def chan(m):
    return slice(m * C, (m + 1) * C)


def pair_kernel(
    table_ref, pos_ref, feat_ref, center_ref, nbr_ref, count_ref,
    emb_ref, value_ref, env_ref, path_ref, latent_ref, gate_ref, final_ref, out_ref,
    site_ref, own_ref, ghost_ref,
    w_emb, w_ve, w_ge, w_fin, w_finb, w_lat, w_latb, w_b1, w_b0, w_embb, w_path, w_out,
    tab_feat, tab_pos, tab_pos3, tab_own,
    hot, hot_t, near, slot_s, geo, harm, basis_s,
    x_s, xh_s, xl_s, d0_s, d1_s, v_s, g_s, e0_s, e1_s, t1_s, t2_s,
    dx_s, dv_s, dg_s, dg0_s, dt1_s, dt2_s, k1_s, k2_s, j1_s, j2_s, dy_s, eps_s,
    big_g, big_h, work, msg_h, msg_l, acc, cat, acc_own, acc_near,
):
    pairs = center_ref.shape[1]
    atoms = pos_ref.shape[1]
    T = TILE
    steps = pairs // T

    stage = pl.program_id(0)

    @pl.when(stage == 0)
    def _():
        emb = emb_ref[...].T
        emb_h = hi(emb)
        emb_l = emb - emb_h
        w_emb[...] = jnp.concatenate(
            [
                jnp.concatenate([emb_h, emb_h[2 * C :]], 0),
                jnp.concatenate([emb_l, jnp.zeros((8, C), f32)], 0),
            ],
            1,
        ).T.astype(bf16)
        low_h = emb_h[2 * C :]
        w_embb[...] = jnp.concatenate(
            [
                jnp.concatenate([low_h, low_h], 1),
                jnp.concatenate([emb_l[2 * C :], jnp.zeros((8, C), f32)], 1),
            ],
            0,
        ).astype(bf16)
        w_ve[...] = forward_stack(jnp.concatenate([value_ref[...], env_ref[0]], 1))
        w_ge[...] = forward_stack(jnp.concatenate([gate_ref[0], env_ref[1]], 1))
        w_b0[...] = backward_stack(jnp.concatenate([env_ref[0], value_ref[...]], 1))
        w_b1[...] = backward_stack(jnp.concatenate([env_ref[1], gate_ref[0]], 1))
        w_fin[...] = forward_stack(final_ref[...])
        w_finb[...] = backward_stack(final_ref[...])
        w_out[...] = jnp.broadcast_to(out_ref[...], (8, C)).T
        for layer in range(2):
            cols = jnp.concatenate([path_ref[:, layer], jnp.ones((1, C), f32)], 0).T
            if layer == 0:
                w_path[...] = cols
            mix = latent_ref[layer].T
            scaled = jnp.concatenate(
                [mix[0:C]] + [mix[chan(i + 1)] * cols[:, i : i + 1] for i in range(3)],
                0,
            )
            first = hi(scaled)
            w_lat[layer] = jnp.concatenate([first, scaled - first], 1).T.astype(bf16)
            w_latb[layer] = backward_stack(scaled)

        tab_pos[...] = jnp.zeros(tab_pos.shape, f32)
        tab_feat[0:C, :] = feat_ref[...]
        tab_feat[14 * C : 15 * C, 128:256] = jnp.zeros((C, 128), bf16)
        for k in range(27):
            half = slice(k % 2 * 128, k % 2 * 128 + 128)
            at = 1 + k // 2
            tab_feat[chan(at), half] = table_ref[k, 0:C, :].astype(bf16)
            for c in range(3):
                tab_pos[c * 16 + at : c * 16 + at + 1, half] = (
                    table_ref[k, C + c : C + c + 1, :] + edge_length * offset(k)[c]
                )
        for c in range(3):
            tab_pos[c * 16 : c * 16 + 1, :] = pos_ref[c : c + 1, :]
        for i, part in enumerate(thirds(tab_pos[...])):
            tab_pos3[i * 48 : (i + 1) * 48, :] = part.astype(bf16)
        tab_own[0:C, :] = feat_ref[...]
        tab_own[C : C + 16, :] = jnp.concatenate(
            list(thirds(pos_ref[...])) + [jnp.zeros((7, atoms), f32)], 0
        ).astype(bf16)

    def span(t):
        return slice(t * T, (t + 1) * T)

    def live_at(t):
        at = lax.broadcasted_iota(jnp.int32, (1, T), 1) + t * T
        return jnp.where(at < jnp.broadcast_to(count_ref[...], (1, T)), 1.0, 0.0)

    def scatter(t):
        many = GROUP
        if t % many == many - 1:
            at = slice((t + 1 - many) * T, (t + 1) * T)
            late = t % RING
            held = slice((late + 1 - many) * T, (late + 1) * T)
            add = dot(msg_h[:, held], hot[at, :]) + dot(msg_l[:, held], hot[at, :])
            if t == many - 1:
                acc[...] = add
            else:
                acc[...] += add

    def gather(t):
        return dot(cat[...], hot_t[:, span(t)])

    def put(m, t, x):
        first, second = halves(x)
        msg_h[chan(m), span(t % RING)] = first
        msg_l[chan(m), span(t % RING)] = second

    def make_cat():
        first, second = halves(acc[...])
        cat[:, 0:atoms] = first
        cat[:, atoms : 2 * atoms] = second

    def spread_latent(xh, xl, scalars):
        split = [halves(s) for s in scalars]
        high = jnp.concatenate([xh] + [s[0] for s in split], 0)
        low = jnp.concatenate([xl] + [s[1] for s in split], 0)
        return high, low

    def latent(layer, high, low):
        both = dot(w_lat[layer], high)
        return both[0:C] + both[C:] + dot(w_lat[layer, 0:C], low)

    def run(phase):
        gens = [phase(t) for t in range(steps)]
        done = 0
        tick = 0
        alive = [True] * steps
        while any(alive):
            for t in range(steps):
                if alive[t] and tick >= t * SKEW:
                    try:
                        next(gens[t])
                    except StopIteration:
                        alive[t] = False
            tick += 1

    def row(m, at):
        return harm[m : m + 1, at]

    def phase_a(t):
        at = span(t)
        nbr = nbr_ref[:, at]
        rest = jnp.bitwise_and(nbr, 255)
        slot = jnp.right_shift(nbr, 8)
        r = (
            lax.broadcasted_iota(jnp.int32, (256, T), 0) == jnp.broadcast_to(rest, (256, T))
        ).astype(bf16)
        near[:, at] = r
        s = jnp.where(
            lax.broadcasted_iota(jnp.int32, (16, T), 0) == jnp.broadcast_to(slot, (16, T)), 1.0, 0.0
        )
        slot_s[:, at] = s
        own = (
            lax.broadcasted_iota(jnp.int32, (atoms, T), 0)
            == jnp.broadcast_to(center_ref[:, at], (atoms, T))
        ).astype(f32)
        hot_t[0:atoms, at] = own.astype(bf16)
        hot_t[atoms : 2 * atoms, at] = own.astype(bf16)
        hot[at, :] = own.T.astype(bf16)
        yield
        found = dot(tab_own[...], hot_t[0:atoms, at])
        far = dot(tab_pos3[...], near[:, at])
        yield
        pos_i = found[C : C + 3] + found[C + 3 : C + 6] + found[C + 6 : C + 9]
        far = far[0:48] + far[48:96] + far[96:144]
        pos_j = jnp.concatenate(
            [jnp.sum(far[c * 16 : c * 16 + 16] * s, 0, keepdims=True) for c in range(3)], 0
        )
        feat_i = found[0:C].astype(bf16)
        feat_j = jnp.zeros((C, T), f32)
        for k0 in range(0, 15, 5):
            got = dot(tab_feat[k0 * C : (k0 + 5) * C, :], near[:, at])
            for k in range(5):
                feat_j = feat_j + got[chan(k)] * s[k0 + k : k0 + k + 1]
        yield
        d = pos_j - pos_i
        rho = jnp.sqrt(jnp.sum(d * d, 0, keepdims=True) + 1.0)
        inv = 1.0 / rho
        u = d * inv
        ux, uy, uz = u[0:1], u[1:2], u[2:3]
        y = [
            None, ux, uy, uz,
            root_three * ux * uy,
            root_three * uy * uz,
            root_three * uz * ux,
            (root_three * 0.5) * (ux * ux - uy * uy),
            0.5 * (2.0 * uz * uz - ux * ux - uy * uy),
        ]
        for m in range(1, 9):
            harm[m : m + 1, at] = y[m]
        geo[0:3, at] = u
        geo[3:4, at] = rho
        mu = lax.broadcasted_iota(jnp.int32, (8, T), 0).astype(f32) * 1.25
        z = rho - mu
        basis = jnp.exp(-0.5 * z * z)
        basis_s[:, at] = basis * z
        joined = jnp.concatenate(
            [
                feat_i,
                feat_j.astype(bf16),
                jnp.concatenate([basis, basis - hi(basis)], 0).astype(bf16),
            ],
            0,
        )
        yield
        pre = dot(w_emb[...], joined)
        yield
        pre = pre[0:C] + pre[C:]
        sg = sigmoid(pre)
        x = pre * sg
        d0_s[:, at] = sg * (1.0 + pre * (1.0 - sg))
        xh, xl = halves(x)
        x_s[:, at] = x
        xh_s[:, at] = xh
        xl_s[:, at] = xl
        yield
        ve = dot(w_ve[...], jnp.concatenate([xh, xl, xh], 0))
        yield
        v_s[:, at] = ve[0:C]
        e = ve[C:] * (env_scale * live_at(t))
        e0_s[:, at] = e
        put(0, t, e)
        for m in range(1, 9):
            put(m, t, e * row(m, at))
        yield
        scatter(t)

    def phase_b(t):
        at = span(t)
        big_g[:, at] = gather(t)
        yield
        g0 = big_g[chan(0), at]
        t1 = big_g[chan(1), at] * row(1, at)
        for m in range(2, 4):
            t1 = t1 + big_g[chan(m), at] * row(m, at)
        t2 = big_g[chan(4), at] * row(4, at)
        for m in range(5, 9):
            t2 = t2 + big_g[chan(m), at] * row(m, at)
        t1_s[:, at] = t1
        t2_s[:, at] = t2
        v = v_s[:, at]
        high, low = spread_latent(xh_s[:, at], xl_s[:, at], [v * g0, v * t1, v * t2])
        yield
        pre = latent(0, high, low)
        yield
        sg = sigmoid(pre)
        x = x_s[:, at] + pre * sg
        d1_s[:, at] = sg * (1.0 + pre * (1.0 - sg))
        xh, xl = halves(x)
        x_s[:, at] = x
        xh_s[:, at] = xh
        xl_s[:, at] = xl
        yield
        ge = dot(w_ge[...], jnp.concatenate([xh, xl, xh], 0))
        yield
        g_s[:, at] = ge[0:C]
        e = ge[C:] * (env_scale * live_at(t))
        e1_s[:, at] = e
        put(0, t, e)
        for m in range(1, 9):
            put(m, t, e * row(m, at))
        yield
        scatter(t)

    def path(i):
        return w_path[:, i : i + 1]

    def phase_c(t):
        at = span(t)
        big_h[:, at] = gather(t)
        yield

        def sums(low, high):
            a = big_g[chan(low), at] * big_h[chan(low), at]
            b = big_h[chan(low), at] * row(low, at)
            for m in range(low + 1, high):
                h = big_h[chan(m), at]
                a = a + big_g[chan(m), at] * h
                b = b + h * row(m, at)
            return a, b

        a1, b1 = sums(1, 4)
        a2, b2 = sums(4, 9)
        g0 = big_g[chan(0), at]
        c0 = path(0) * g0 + path(1) * t1_s[:, at] + path(2) * t2_s[:, at]
        h4 = path(4) * g0
        h6 = path(6) * g0
        p0 = c0 * big_h[chan(0), at]
        p1 = path(3) * a1 + h4 * b1
        p2 = path(5) * a2 + h6 * b2
        gv = g_s[:, at] * v_s[:, at]
        high, low = spread_latent(xh_s[:, at], xl_s[:, at], [gv * p0, gv * p1, gv * p2])
        yield
        pre = latent(1, high, low)
        yield
        sg = sigmoid(pre)
        x = x_s[:, at] + pre * sg
        d2 = sg * (1.0 + pre * (1.0 - sg))
        x = stacked(x)
        yield
        hid = dot(w_fin[...], x)
        yield
        sg = sigmoid(hid)
        live = live_at(t)
        ow = w_out[:, 0:1]
        eps_s[:, at] = jnp.sum(fold(ow * (hid * sg)), 0, keepdims=True) * live
        dhid = (ow * live) * (sg * (1.0 + hid * (1.0 - sg)))
        dhid = stacked(dhid)
        yield
        dx = dot(w_finb[...], dhid)
        yield
        dpre = stacked(dx * d2)
        yield
        dm = dot(w_latb[1], dpre)
        yield
        dx_s[:, at] = dx + dm[0:C]
        ds0, ds1, ds2 = dm[chan(1)], dm[chan(2)], dm[chan(3)]
        dgv = ds0 * p0 + ds1 * p1 + ds2 * p2
        v = v_s[:, at]
        g = g_s[:, at]
        dg_s[:, at] = dgv * v
        dv_s[:, at] = dgv * g
        u0 = ds0 * gv
        u1 = ds1 * gv
        u2 = ds2 * gv
        k1 = u1 * path(3)
        k2 = u2 * path(5)
        j1 = u1 * h4
        j2 = u2 * h6
        k1_s[:, at] = k1
        k2_s[:, at] = k2
        j1_s[:, at] = j1
        j2_s[:, at] = j2
        uh = u0 * big_h[chan(0), at]
        dg0_s[:, at] = uh * path(0) + u1 * path(4) * b1 + u2 * path(6) * b2
        dt1_s[:, at] = uh * path(1)
        dt2_s[:, at] = uh * path(2)
        put(0, t, u0 * c0)
        for m in range(1, 9):
            k, j = (k1, j1) if m < 4 else (k2, j2)
            put(m, t, k * big_g[chan(m), at] + j * row(m, at))
        yield
        scatter(t)

    def phase_d(t):
        at = span(t)
        wat = span(t % RING)
        work[:, wat] = gather(t)
        yield
        de = work[chan(0), wat]
        for m in range(1, 9):
            de = de + work[chan(m), wat] * row(m, at)
        de = de * (env_scale * live_at(t))
        deh, del_ = halves(de)
        dgh, dgl = halves(dg_s[:, at])
        pair = jnp.concatenate([deh, dgh, del_, dgl, deh, dgh], 0)
        yield
        dx = dot(w_b1[...], pair)
        yield
        dx = dx_s[:, at] + dx
        dpre = stacked(dx * d1_s[:, at])
        yield
        dm = dot(w_latb[0], dpre)
        yield
        dx_s[:, at] = dx + dm[0:C]
        ds0, ds1, ds2 = dm[chan(1)], dm[chan(2)], dm[chan(3)]
        v = v_s[:, at]
        dv_s[:, at] += ds0 * big_g[chan(0), at] + ds1 * t1_s[:, at] + ds2 * t2_s[:, at]
        dt1 = dt1_s[:, at] + ds1 * v
        dt2 = dt2_s[:, at] + ds2 * v
        put(0, t, dg0_s[:, at] + ds0 * v)
        e = e1_s[:, at]
        for m in range(1, 9):
            if m < 4:
                k, j, dt = k1_s[:, at], j1_s[:, at], dt1
            else:
                k, j, dt = k2_s[:, at], j2_s[:, at], dt2
            h = big_h[chan(m), at]
            dy_s[8 * m : 8 * m + 8, at] = fold(
                j * h + dt * big_g[chan(m), at] + e * work[chan(m), wat]
            )
            put(m, t, k * h + dt * row(m, at))
        yield
        scatter(t)

    def phase_e(t):
        at = span(t)
        wat = span(t % RING)
        work[:, wat] = gather(t)
        yield
        de = work[chan(0), wat]
        for m in range(1, 9):
            de = de + work[chan(m), wat] * row(m, at)
        de = de * (env_scale * live_at(t))
        deh, del_ = halves(de)
        dvh, dvl = halves(dv_s[:, at])
        pair = jnp.concatenate([deh, dvh, del_, dvl, deh, dvh], 0)
        e = e0_s[:, at]
        dy = [None]
        for m in range(1, 9):
            part = dy_s[8 * m : 8 * m + 8, at] + fold(e * work[chan(m), wat])
            dy.append(jnp.sum(part, 0, keepdims=True))
        yield
        dx = dot(w_b0[...], pair)
        yield
        dpre = jnp.concatenate(halves((dx_s[:, at] + dx) * d0_s[:, at]), 0)
        yield
        dbasis = dot(w_embb[...], dpre)
        dbasis = dbasis[0:8] + dbasis[8:16]
        yield
        drho = -jnp.sum(dbasis * basis_s[:, at], 0, keepdims=True)
        u = geo[0:3, at]
        rho = geo[3:4, at]
        inv = 1.0 / rho
        ux, uy, uz = u[0:1], u[1:2], u[2:3]
        dux = dy[1] + root_three * (uy * dy[4] + uz * dy[6] + ux * dy[7]) - ux * dy[8]
        duy = dy[2] + root_three * (ux * dy[4] + uz * dy[5] - uy * dy[7]) - uy * dy[8]
        duz = dy[3] + root_three * (uy * dy[5] + ux * dy[6]) + 2.0 * (uz * dy[8])
        along = drho - (dux * ux + duy * uy + duz * uz) * inv
        dd = [dux * inv + ux * along, duy * inv + uy * along, duz * inv + uz * along]
        rows = jnp.concatenate(dd + [eps_s[:, at]], 0)
        first = hi(rows)
        rest = rows - first
        second = hi(rest)
        rows = jnp.concatenate(
            [first, second, rest - second, jnp.zeros((4, T), f32)], 0
        ).astype(bf16)
        s = slot_s[:, at]
        spread = jnp.concatenate([s * dd[c] for c in range(3)], 0)
        first = hi(spread)
        spread = jnp.concatenate([first, spread - first], 0).astype(bf16)
        yield
        acc_own[...] += dot(rows, hot[at, :])
        acc_near[...] += dot_nt(spread, near[:, at])

    @pl.when(stage == 0)
    def _():
        run(phase_a)
        make_cat()

    for number, phase in ((1, phase_b), (2, phase_c), (3, phase_d)):

        @pl.when(stage == number)
        def _(phase=phase):
            run(phase)
            make_cat()

    @pl.when(stage == 4)
    def _():
        acc_own[...] = jnp.zeros(acc_own.shape, f32)
        acc_near[...] = jnp.zeros(acc_near.shape, f32)
        run(phase_e)
        own = acc_own[0:4, :] + acc_own[4:8, :] + acc_own[8:12, :]
        site_ref[...] = own[3:4, :]
        ghosts = acc_near[0:48, :] + acc_near[48:96, :]
        for c in range(3):
            own_ref[c : c + 1, :] = ghosts[c * 16 : c * 16 + 1] - own[c : c + 1]
        ghost_ref[...] = jnp.zeros(ghost_ref.shape, f32)
        for k in range(27):
            half = slice(k % 2 * 128, k % 2 * 128 + 128)
            for c in range(3):
                at = c * 16 + 1 + k // 2
                ghost_ref[k, c : c + 1, :] = ghosts[at : at + 1, half]


def pair_grads(table, positions, features, center, nbr, count, params):
    pairs = center.shape[1]
    atoms = positions.shape[1]
    T = TILE
    emb, value, env, path, latent, *rest = params
    params = (emb.T, value, env, path.transpose(1, 0, 2), latent.transpose(0, 2, 1), *rest)

    def wide(rows, dtype=f32):
        return pltpu.VMEM((rows, pairs), dtype)

    scratch = [
        pltpu.VMEM((128, 144), bf16),
        pltpu.VMEM((128, 192), bf16),
        pltpu.VMEM((128, 192), bf16),
        pltpu.VMEM((64, 192), bf16),
        pltpu.VMEM((64, 192), bf16),
        pltpu.VMEM((2, 128, 256), bf16),
        pltpu.VMEM((2, 256, 192), bf16),
        pltpu.VMEM((64, 384), bf16),
        pltpu.VMEM((64, 384), bf16),
        pltpu.VMEM((16, 128), bf16),
        pltpu.VMEM((64, 8), f32),
        pltpu.VMEM((64, 8), f32),
        pltpu.VMEM((15 * 64, 256), bf16),
        pltpu.VMEM((48, 256), f32),
        pltpu.VMEM((144, 256), bf16),
        pltpu.VMEM((80, atoms), bf16),
        pltpu.VMEM((pairs, atoms), bf16),
        wide(2 * atoms, bf16),
        wide(256, bf16),
        wide(16),
        wide(8),
        wide(16),
        wide(8),
        wide(64),
        wide(64, bf16),
        wide(64, bf16),
    ]
    scratch += [wide(64)] * 18
    scratch += [wide(72), wide(1)]
    scratch += [
        wide(576),
        wide(576),
        pltpu.VMEM((576, RING * T), f32),
        pltpu.VMEM((576, RING * T), bf16),
        pltpu.VMEM((576, RING * T), bf16),
        pltpu.VMEM((576, atoms), f32),
        pltpu.VMEM((576, 2 * atoms), bf16),
        pltpu.VMEM((16, atoms), f32),
        pltpu.VMEM((96, 256), f32),
    ]
    vmem = pl.BlockSpec(memory_space=pltpu.VMEM)
    return pl.pallas_call(
        pair_kernel,
        out_shape=(
            jax.ShapeDtypeStruct((1, atoms), f32),
            jax.ShapeDtypeStruct((3, atoms), f32),
            jax.ShapeDtypeStruct((27, 8, 128), f32),
        ),
        grid=(5,),
        in_specs=[vmem] * 14,
        out_specs=(vmem, vmem, vmem),
        scratch_shapes=scratch,
        compiler_params=pltpu.CompilerParams(vmem_limit_bytes=60 * 1024 * 1024),
        cost_estimate=pl.CostEstimate(flops=40 * 10**9, bytes_accessed=10**6, transcendentals=10**6),
    )(table, positions, features, center, nbr, count, *params)


def local(
    positions, features, ghost_rows, pair_center, pair_nbr, pair_count,
    emb_weight, value_weight, env_weight, path_weight, latent_weight, gate_weight,
    final_weight, out_weight,
):
    rows = ghost_rows.reshape(1, -1)
    table = halo(positions, features, rows)
    site, own, ghost = pair_grads(
        table, positions, features,
        pair_center.reshape(1, -1), pair_nbr.reshape(1, -1), pair_count.reshape(1, 1),
        (emb_weight, value_weight, env_weight, path_weight, latent_weight, gate_weight,
         final_weight, out_weight.reshape(1, -1)),
    )
    forces = give_back(ghost, own, rows)
    return (site.reshape(-1), forces)


def solution(mesh):
    placed = (
        P(None, axes),
        P(None, axes),
        P(axes),
        P(axes),
        P(axes),
        P(axes),
    ) + (P(),) * 8
    return jax.shard_map(
        local,
        mesh=mesh,
        in_specs=placed,
        out_specs=(P(axes), P(None, axes)),
        check_vma=False,
    )
```
